32 devices in a mesh: gx: 8 (over y, x, core), gy: 4 (over z).
Axes of the slice: x: 2, y: 2, z: 4, core: 2. Of those that a mesh axis runs over, the one named last changes fastest.
Arguments:
- operator_blocks: float32 [16, 8, 12, 7, 64, 64], P('gx', 'gy'), may hold values from -1 to 13, as said below
- start_block: float32 [16, 8, 12, 64, 16], P('gx', 'gy'), may hold values from -4000 to 4000
Outputs:
- orthonormal: float32 [16, 8, 12, 64, 80], P('gx', 'gy')
- triangle: float32 [80, 80], replicated
The draws below stay inside these ranges and needn't reach their ends.
Inputs may be any that keep to these rules, and one draw needn't show every extreme that they name: `operator_blocks`: the own block of every element is diagonally dominant; other entries are small.
All inputs are finite; a program needn't handle non-finite values.
Results may differ from the reference program's by a relative error of at most 0.0003.
Values sent between devices are 32-bit elements; how exact they have to be, the bound alone decides.
A program may use at most 64 MiB of HBM per device.

```python
import jax
import jax.numpy as jnp
from jax import lax

P_SIZE = 64
RHS = 16
STEPS = 4
COLS = 80
NX = 16
NY = 8
NZ = 12


def draw_operator_blocks(key, part):
    first, second = jax.random.split(jax.random.fold_in(key, 11), 2)
    spread = 0.4 / P_SIZE ** 0.5
    noise = spread * jnp.clip(jax.random.normal(first, (NX, NY, NZ, 7, P_SIZE, P_SIZE), jnp.float32), -4.0, 4.0)
    diagonal = jax.random.uniform(second, (NX, NY, NZ, P_SIZE), jnp.float32, 4.0, 12.0)
    identity = jnp.eye(P_SIZE, dtype=jnp.float32)
    own = noise[:, :, :, 0] + diagonal[..., :, None] * identity
    return noise.at[:, :, :, 0].set(own)


def draw_start_block(key, part):
    keys = jax.random.split(jax.random.fold_in(key, 23), 3)
    logten = jnp.log(10.0)
    rows = jnp.exp(logten * jax.random.uniform(keys[1], (NX, NY, NZ, P_SIZE, 1), jnp.float32))
    columns = jnp.exp(logten * jax.random.uniform(keys[2], (RHS,), jnp.float32))
    along_x = jnp.arange(NX, dtype=jnp.float32) / max(NX - 1, 1)
    along_y = jnp.arange(NY, dtype=jnp.float32) / max(NY - 1, 1)
    trend = jnp.exp(jnp.log(3.0) * (along_x[:, None] + along_y[None, :]))
    values = jnp.clip(jax.random.normal(keys[0], (NX, NY, NZ, P_SIZE, RHS), jnp.float32), -4.0, 4.0)
    return values * rows * columns * trend[:, :, None, None, None]


def setup_inputs(seed: int = 0) -> dict:
    key_list = jax.random.split(jax.random.key(seed), 3)
    return {
        "operator_blocks": draw_operator_blocks(jax.random.fold_in(key_list[2], 71), 0),
        "start_block": draw_start_block(jax.random.fold_in(key_list[2], 71), 0),
    }


def apply_operator(vector, operator_blocks):
    padded = jnp.pad(vector, ((1, 1), (1, 1), (1, 1), (0, 0), (0, 0)))
    stacked = jnp.stack([vector, padded[:-2, 1:-1, 1:-1], padded[2:, 1:-1, 1:-1], padded[1:-1, :-2, 1:-1], padded[1:-1, 2:, 1:-1], padded[1:-1, 1:-1, :-2], padded[1:-1, 1:-1, 2:]], axis=3)
    return jnp.einsum('xyzfij,xyzfjr->xyzir', operator_blocks, stacked, precision=lax.Precision.HIGHEST)

def reference(operator_blocks, start_block):
    previous = start_block
    current = (apply_operator(previous, operator_blocks) - 8.0 * previous) / 6.0
    pieces = [previous, current]
    for index in range(STEPS - 1):
        following = 2.0 * (apply_operator(current, operator_blocks) - 8.0 * current) / 6.0 - previous
        previous, current = (current, following)
        pieces.append(following)
    basis = jnp.concatenate(pieces, axis=-1)
    tall = basis.reshape(-1, COLS)
    factor_q, factor_r = jnp.linalg.qr(tall)
    signs = jnp.where(jnp.diagonal(factor_r) >= 0, 1.0, -1.0).astype(factor_r.dtype)
    orthonormal = (factor_q * signs[None, :]).reshape(basis.shape)
    triangle = factor_r * signs[:, None]
    return (orthonormal, triangle)
```

```python
import functools

import jax
import jax.numpy as jnp
from jax import lax
from jax.experimental import pallas as pl
from jax.experimental.pallas import tpu as pltpu
from jax.sharding import PartitionSpec as P

STEPS = 4
F32 = jnp.float32
BF16 = jnp.bfloat16
NT = (((1,), (1,)), ((), ()))
MESH = pl.DeviceIdType.MESH


def limbs(value):
    high = value.astype(BF16)
    return high, (value - high.astype(F32)).astype(BF16)


def dot_nt(left, right):
    return lax.dot_general(left, right, NT, preferred_element_type=F32)


def chunk_of(count, most):
    return max(size for size in range(1, most + 1) if count % size == 0)


def in_place_factor(blocks):
    width = 8 * len(blocks)
    lane = lax.broadcasted_iota(jnp.int32, blocks[0].shape, 1)
    rows = lax.broadcasted_iota(jnp.int32, blocks[0].shape, 0)
    blocks = list(blocks)
    for j in range(width):
        first, inside = divmod(j, 8)
        pivot_row = blocks[first][inside : inside + 1, :]
        inverse = 1.0 / pivot_row[:, j : j + 1]
        scaled = jnp.where(lane[:1] == j, 1.0, pivot_row) * inverse
        for b in range(first, len(blocks)):
            column = blocks[b][:, j : j + 1]
            kept = jnp.where(lane == j, 0.0, blocks[b])
            update = kept - column * scaled
            if b == first:
                update = jnp.where(rows > inside, update, blocks[b])
            blocks[b] = update
    return blocks


def kernel(dims, blocks_hbm, start_ref, ortho_hbm, tri_ref, raw, weights, tall, limb, vert,
           partial, rx, ry, gram_x, gram_y, ortho, raw_sem, ortho_sem, send_x, recv_x, send_y,
           recv_y, send_gx, recv_gx, send_gy, recv_gy):
    n_gx, n_gy, nx, ny, nz, unk, rhs = dims
    pairs = nz // 2
    wide = 2 * unk
    cols = (STEPS + 1) * rhs
    gx, gy = lax.axis_index("gx"), lax.axis_index("gy")
    columns = [(x, y) for x in range(nx) for y in range(ny)]
    chunk = chunk_of(pairs, 3)

    def raw_copy(c):
        x, y = columns[c]
        return pltpu.make_async_copy(blocks_hbm.at[x, y], raw.at[c], raw_sem.at[c])

    for c in range(len(columns)):
        raw_copy(c).start()

    barrier = pltpu.get_barrier_semaphore()
    for d in range(1, n_gx):
        pl.semaphore_signal(barrier, inc=1, device_id={"gx": lax.rem(gx + d, n_gx)}, device_id_type=MESH)
    for d in range(1, n_gy):
        pl.semaphore_signal(barrier, inc=1, device_id={"gy": lax.rem(gy + d, n_gy)}, device_id_type=MESH)

    def store_basis(k, c, m, value):
        x, y = columns[c]
        tall[k, x, y, m] = value
        high, low = limbs(value)
        limb[c, m, rhs * k : rhs * (k + 1)] = high
        limb[c, m, cols + rhs * k : cols + rhs * (k + 1)] = low
        if k < STEPS:
            both = jnp.concatenate([high, low], axis=0)
            vert[c, m, :, 0:unk] = both[:, 0:unk]
            vert[c, m + 2, :, unk:wide] = both[:, unk:wide]

    def borders(c):
        x, y = columns[c]
        return [("gx", 0, x == 0), ("gx", 1, x == nx - 1), ("gy", 0, y == 0), ("gy", 1, y == ny - 1)]

    def has(axis, side):
        here, count = (gx, n_gx) if axis == "gx" else (gy, n_gy)
        return here > 0 if side == 0 else here < count - 1

    def halo_copy(k, c, axis, side):
        x, y = columns[c]
        if axis == "gx":
            target, land, at, ss, rs = gx, rx, y, send_x, recv_x
        else:
            target, land, at, ss, rs = gy, ry, x, send_y, recv_y
        target = target - 1 if side == 0 else target + 1
        return pltpu.make_async_remote_copy(
            src_ref=tall.at[k, x, y], dst_ref=land.at[k, 1 - side, at],
            send_sem=ss.at[k, side, at], recv_sem=rs.at[k, 1 - side, at],
            device_id={axis: target}, device_id_type=MESH)

    def halo_wait(k, c, axis, side):
        x, y = columns[c]
        if axis == "gx":
            target, land, at, ss, rs = gx, rx, y, send_x, recv_x
        else:
            target, land, at, ss, rs = gy, ry, x, send_y, recv_y
        target = target - 1 if side == 0 else target + 1
        pltpu.make_async_remote_copy(
            src_ref=tall.at[k, x, y], dst_ref=land.at[k, side, at],
            send_sem=ss.at[k, side, at], recv_sem=rs.at[k, side, at],
            device_id={axis: target}, device_id_type=MESH).wait_recv()

    def send_column(k, c):
        for axis, side, edge in borders(c):
            if edge:
                @pl.when(has(axis, side))
                def _():
                    halo_copy(k, c, axis, side).start()

    for c, (x, y) in enumerate(columns):
        vert[c, 1, :, unk:wide] = jnp.zeros((2 * rhs, unk), BF16)
        vert[c, pairs, :, 0:unk] = jnp.zeros((2 * rhs, unk), BF16)
        for m in range(pairs):
            store_basis(0, c, m, jnp.concatenate([start_ref[x, y, 2 * m], start_ref[x, y, 2 * m + 1]], axis=1))
    for axis, land in (("gx", rx), ("gy", ry)):
        for side in (0, 1):
            @pl.when(jnp.logical_not(has(axis, side)))
            def _():
                for k in range(STEPS):
                    land[k, side] = jnp.zeros(land.shape[2:], F32)

    pl.semaphore_wait(barrier, n_gx + n_gy - 2)
    for c in range(len(columns)):
        send_column(0, c)

    def order(c):
        marks = [edge for _, _, edge in borders(c)]
        near = [d for d in range(4) if not marks[d]]
        far = [d for d in range(4) if marks[d]]
        return near, far

    zeros = jnp.zeros((unk, unk), F32)

    def prepare(c):
        near, far = order(c)

        def body(m, carry):
            low, up = raw.at[c, 2 * m], raw.at[c, 2 * m + 1]
            pieces = [
                ((low[0], low[6]), (up[5], up[0])),
                ((zeros, low[5]), (up[6], zeros)),
            ]
            for d in near + far:
                pieces.append(((low[1 + d], zeros), (zeros, up[1 + d])))
            for at, halves in enumerate(pieces):
                for half, (left, right) in enumerate(halves):
                    high, rest = limbs(jnp.concatenate([left, right], axis=1))
                    lanes = slice(at * wide, (at + 1) * wide)
                    weights[c, m, half * unk : (half + 1) * unk, lanes] = high
                    weights[c, m, wide + half * unk : wide + (half + 1) * unk, lanes] = rest
            return carry

        lax.fori_loop(0, pairs, body, 0)

    def fold(product):
        rows = product[0:rhs] + product[rhs : 2 * rhs]
        return rows[:, 0:wide] + rows[:, wide : 2 * wide]

    def rows_of(k, c, m):
        return jnp.concatenate(
            [limb[c, m, rhs * k : rhs * (k + 1)], limb[c, m, cols + rhs * k : cols + rhs * (k + 1)]], axis=0)

    def neighbour(c, d):
        x, y = columns[c]
        step = ((-1, 0), (1, 0), (0, -1), (0, 1))[d]
        return columns.index((x + step[0], y + step[1]))

    def near_part(k, c):
        near, _ = order(c)

        def body(i, carry):
            for s in range(chunk):
                m = i * chunk + s
                pieces = [rows_of(k, c, m), vert[c, m + 1]]
                pieces += [rows_of(k, neighbour(c, d), m) for d in near]
                left = jnp.concatenate(pieces, axis=1)
                partial[c, m] = fold(dot_nt(left, weights[c, m, :, 0 : left.shape[1]]))
            return carry

        lax.fori_loop(0, pairs // chunk, body, 0)

    def far_part(k, c):
        x, y = columns[c]
        near, far = order(c)
        for d in far:
            axis, side, _ = borders(c)[d]

            @pl.when(has(axis, side))
            def _():
                halo_wait(k, c, axis, side)

        def body(i, carry):
            for s in range(chunk):
                m = i * chunk + s
                pieces = []
                for d in far:
                    value = rx[k, d, y, m] if d < 2 else ry[k, d - 2, x, m]
                    pieces.append(jnp.concatenate(limbs(value), axis=0))
                applied = partial[c, m]
                if pieces:
                    left = jnp.concatenate(pieces, axis=1)
                    begin = (2 + len(near)) * wide
                    applied = applied + fold(dot_nt(left, weights[c, m, :, begin : begin + left.shape[1]]))
                current = tall[k, x, y, m]
                if k == 0:
                    following = (applied - 8.0 * current) * (1.0 / 6.0)
                else:
                    following = (applied - 8.0 * current) * (2.0 / 6.0) - tall[k - 1, x, y, m]
                store_basis(k + 1, c, m, following)
            return carry

        lax.fori_loop(0, pairs // chunk, body, 0)

    def gram_rows(k):
        count = rhs * (k + 1)
        total_high = jnp.zeros((2 * rhs, count), F32)
        total_low = jnp.zeros((2 * rhs, count), F32)
        for c in range(len(columns)):
            for m in range(0, pairs, 2):
                span = range(m, min(m + 2, pairs))
                left = jnp.concatenate([rows_of(k, c, q) for q in span], axis=1)
                high = jnp.concatenate([limb[c, q, 0:count] for q in span], axis=1)
                low = jnp.concatenate([limb[c, q, cols : cols + count] for q in span], axis=1)
                total_high += dot_nt(left, high)
                total_low += dot_nt(left, low)
        total = total_high + total_low
        gram_x[gx, rhs * k : rhs * (k + 1), 0:count] = total[0:rhs] + total[rhs : 2 * rhs]

    gram_x[gx] = jnp.zeros(gram_x.shape[1:], F32)
    for c in range(len(columns)):
        raw_copy(c).wait()
        prepare(c)
    for k in range(STEPS):
        for c in range(len(columns)):
            near_part(k, c)
        gram_rows(k)
        for c in range(len(columns)):
            far_part(k, c)
            if k + 1 < STEPS:
                send_column(k + 1, c)
    gram_rows(STEPS)

    def broadcast(axis, here, count, slots, send, recv):
        def copy(d):
            return pltpu.make_async_remote_copy(
                src_ref=slots.at[here], dst_ref=slots.at[here], send_sem=send.at[d], recv_sem=recv.at[here],
                device_id={axis: lax.rem(here + d, count)}, device_id_type=MESH)

        for d in range(1, count):
            copy(d).start()
        for d in range(1, count):
            source = lax.rem(here + d, count)
            pltpu.make_async_remote_copy(
                src_ref=slots.at[source], dst_ref=slots.at[source], send_sem=send.at[d], recv_sem=recv.at[source],
                device_id={axis: source}, device_id_type=MESH).wait_recv()
        total = slots[0]
        for i in range(1, count):
            total = total + slots[i]
        return total, copy

    total, copy_x = broadcast("gx", gx, n_gx, gram_x, send_gx, recv_gx)
    gram_y[gy] = total
    total, copy_y = broadcast("gy", gy, n_gy, gram_y, send_gy, recv_gy)

    rows = lax.broadcasted_iota(jnp.int32, (cols, wide), 0)
    lane = lax.broadcasted_iota(jnp.int32, (cols, wide), 1)
    square = jnp.concatenate([total, jnp.zeros((wide - cols, wide), F32)], axis=0)
    whole = jnp.where(lane > rows, square.T[0:cols], total)
    factored = in_place_factor([whole[8 * b : 8 * b + 8] for b in range(cols // 8)])
    factored = jnp.concatenate(factored, axis=0)
    diagonal = jnp.sum(jnp.where(lane == rows, factored, 0.0), axis=1, keepdims=True)
    root = jnp.sqrt(diagonal)
    scale = 1.0 / root
    upper = jnp.where(lane > rows, factored * scale, 0.0) + jnp.where(lane == rows, root, 0.0)
    tri_ref[...] = upper[:, 0:cols]
    inverse = (jnp.where(lane < rows, factored, 0.0) + jnp.where(lane == rows, 1.0, 0.0)) * scale
    inverse = jnp.concatenate([inverse, jnp.zeros((wide - cols, wide), F32)], axis=0)
    inverse_high, inverse_low = limbs(inverse)
    right = jnp.concatenate(
        [jnp.concatenate([inverse_high, inverse_high], axis=1), jnp.concatenate([inverse_low, inverse_low], axis=1)],
        axis=0)

    def ortho_copy(c):
        x, y = columns[c]
        return pltpu.make_async_copy(ortho.at[c], ortho_hbm.at[x, y], ortho_sem.at[c])

    for c, (x, y) in enumerate(columns):
        def body(i, carry):
            for s in range(chunk):
                m = i * chunk + s
                pieces = [tall[k, x, y, m] for k in range(STEPS + 1)]
                block = jnp.concatenate(pieces + [jnp.zeros((wide - cols, wide), F32)], axis=0).T
                product = dot_nt(jnp.concatenate(limbs(block), axis=1), right)
                result = (product[:, 0:wide] + product[:, wide : 2 * wide])[:, 0:cols]
                ortho[c, 2 * m] = result[0:unk]
                ortho[c, 2 * m + 1] = result[unk:wide]
            return carry

        lax.fori_loop(0, pairs // chunk, body, 0)
        ortho_copy(c).start()

    for d in range(1, n_gx):
        copy_x(d).wait_send()
    for d in range(1, n_gy):
        copy_y(d).wait_send()
    for k in range(STEPS):
        for c in range(len(columns)):
            for axis, side, edge in borders(c):
                if edge:
                    @pl.when(has(axis, side))
                    def _():
                        halo_copy(k, c, axis, side).wait_send()
    for c in range(len(columns)):
        ortho_copy(c).wait()


def per_device(operator_blocks, start_block):
    nx, ny, nz, _, unk, _ = operator_blocks.shape
    rhs = start_block.shape[-1]
    n_gx, n_gy = lax.axis_size("gx"), lax.axis_size("gy")
    pairs, wide, cols, count = nz // 2, 2 * unk, (STEPS + 1) * rhs, nx * ny
    assert nz % 2 == 0 and wide == 128 and rhs % 16 == 0 and cols <= wide
    dma = pltpu.SemaphoreType.DMA
    return pl.pallas_call(
        functools.partial(kernel, (n_gx, n_gy, nx, ny, nz, unk, rhs)),
        out_shape=(
            jax.ShapeDtypeStruct((nx, ny, nz, unk, cols), F32),
            jax.ShapeDtypeStruct((cols, cols), F32),
        ),
        in_specs=[pl.BlockSpec(memory_space=pl.ANY), pl.BlockSpec(memory_space=pltpu.VMEM)],
        out_specs=(pl.BlockSpec(memory_space=pl.ANY), pl.BlockSpec(memory_space=pltpu.VMEM)),
        scratch_shapes=[
            pltpu.VMEM((count, nz, 7, unk, unk), F32),
            pltpu.VMEM((count, pairs, 2 * wide, 6 * wide), BF16),
            pltpu.VMEM((STEPS + 1, nx, ny, pairs, rhs, wide), F32),
            pltpu.VMEM((count, pairs, 2 * cols, wide), BF16),
            pltpu.VMEM((count, pairs + 2, 2 * rhs, wide), BF16),
            pltpu.VMEM((count, pairs, rhs, wide), F32),
            pltpu.VMEM((STEPS, 2, ny, pairs, rhs, wide), F32),
            pltpu.VMEM((STEPS, 2, nx, pairs, rhs, wide), F32),
            pltpu.VMEM((n_gx, cols, wide), F32),
            pltpu.VMEM((n_gy, cols, wide), F32),
            pltpu.VMEM((count, nz, unk, cols), F32),
            dma((count,)),
            dma((count,)),
            dma((STEPS, 2, ny)),
            dma((STEPS, 2, ny)),
            dma((STEPS, 2, nx)),
            dma((STEPS, 2, nx)),
            dma((n_gx,)),
            dma((n_gx,)),
            dma((n_gy,)),
            dma((n_gy,)),
        ],
        compiler_params=pltpu.CompilerParams(
            collective_id=0, has_side_effects=True, vmem_limit_bytes=52 * 1024 * 1024
        ),
        cost_estimate=pl.CostEstimate(flops=6_000_000_000, bytes_accessed=16_000_000, transcendentals=0),
    )(operator_blocks, jnp.swapaxes(start_block, -1, -2))


def solution(mesh):
    in_specs = (P("gx", "gy", None, None, None, None), P("gx", "gy", None, None, None))
    out_specs = (P("gx", "gy", None, None, None), P())
    return jax.shard_map(
        per_device, mesh=mesh, in_specs=in_specs, out_specs=out_specs, check_vma=False
    )
```

```python
import functools

import jax
import jax.numpy as jnp
from jax import lax
from jax.experimental import pallas as pl
from jax.experimental.pallas import tpu as pltpu
from jax.sharding import PartitionSpec as P

STEPS = 4
F32 = jnp.float32
BF16 = jnp.bfloat16
NT = (((1,), (1,)), ((), ()))
MESH = pl.DeviceIdType.MESH


def limbs(value):
    high = value.astype(BF16)
    return high, (value - high.astype(F32)).astype(BF16)


def dot_nt(left, right):
    return lax.dot_general(left, right, NT, preferred_element_type=F32)


def chunk_of(count, most):
    return max(size for size in range(1, most + 1) if count % size == 0)


def dot_full(left, right, dims=(((1,), (0,)), ((), ()))):
    return lax.dot_general(left, right, dims, precision=lax.Precision.HIGHEST, preferred_element_type=F32)


def eliminate(blocks, start, stop):
    lane = lax.broadcasted_iota(jnp.int32, blocks[0].shape, 1)
    rows = lax.broadcasted_iota(jnp.int32, blocks[0].shape, 0)
    line = lane[:1]
    blocks = list(blocks)
    for j in range(start, stop, 2):
        first, inside = divmod(j, 8)
        row_0 = blocks[first][inside : inside + 1, :]
        row_1 = blocks[first][inside + 1 : inside + 2, :]
        a, b, c = row_0[:, j : j + 1], row_0[:, j + 1 : j + 2], row_1[:, j + 1 : j + 2]
        inverse = 1.0 / (a * c - b * b)
        unit_0 = jnp.where(line == j, 1.0, jnp.where(line == j + 1, 0.0, row_0))
        unit_1 = jnp.where(line == j + 1, 1.0, jnp.where(line == j, 0.0, row_1))
        scaled_0 = (c * unit_0 - b * unit_1) * inverse
        scaled_1 = (a * unit_1 - b * unit_0) * inverse
        ratio = b / a
        second = jnp.where(line == j, -ratio, row_1 - ratio * row_0)
        pair = jnp.logical_or(lane == j, lane == j + 1)
        for i in range(first, len(blocks)):
            block = blocks[i]
            kept = jnp.where(pair, 0.0, block)
            update = kept - block[:, j : j + 1] * scaled_0 - block[:, j + 1 : j + 2] * scaled_1
            if i == first:
                update = jnp.where(rows > inside + 1, update, jnp.where(rows == inside + 1, second, block))
            blocks[i] = update
    return blocks


def split_factor(blocks):
    factored = jnp.concatenate(blocks, axis=0)
    lane = lax.broadcasted_iota(jnp.int32, factored.shape, 1)
    rows = lax.broadcasted_iota(jnp.int32, factored.shape, 0)
    diagonal = jnp.sum(jnp.where(lane == rows, factored, 0.0), axis=1, keepdims=True)
    root = jnp.sqrt(diagonal)
    scale = 1.0 / root
    upper = jnp.where(lane > rows, factored * scale, jnp.where(lane == rows, root, 0.0))
    inverse = jnp.where(lane < rows, factored * scale, jnp.where(lane == rows, scale, 0.0))
    return upper, inverse


def kernel(dims, blocks_hbm, start_hbm, ortho_hbm, tri_ref, start_ref, raw, weights, tall, limb, vert,
           partial, rx, ry, gram_x, gram_y, turned, ortho, start_sem, raw_sem, ortho_sem, send_x, recv_x,
           send_y, recv_y, send_gx, recv_gx, send_gy, recv_gy):
    n_gx, n_gy, nx, ny, nz, unk, rhs = dims
    pairs = nz // 2
    wide = 2 * unk
    cols = (STEPS + 1) * rhs
    gx, gy = lax.axis_index("gx"), lax.axis_index("gy")
    columns = [(x, y) for x in range(nx) for y in range(ny)]
    chunk = chunk_of(pairs, 3)

    def raw_copy(c):
        x, y = columns[c]
        return pltpu.make_async_copy(blocks_hbm.at[x, y], raw.at[c], raw_sem.at[c])

    start_copy = pltpu.make_async_copy(start_hbm, start_ref, start_sem)
    start_copy.start()
    for c in range(len(columns)):
        raw_copy(c).start()

    barrier = pltpu.get_barrier_semaphore()
    for d in range(1, n_gx):
        pl.semaphore_signal(barrier, inc=1, device_id={"gx": lax.rem(gx + d, n_gx)}, device_id_type=MESH)
    for d in range(1, n_gy):
        pl.semaphore_signal(barrier, inc=1, device_id={"gy": lax.rem(gy + d, n_gy)}, device_id_type=MESH)

    def store_basis(k, c, m, value):
        x, y = columns[c]
        tall[k, x, y, m] = value
        high, low = limbs(value)
        limb[c, m, rhs * k : rhs * (k + 1)] = high
        limb[c, m, cols + rhs * k : cols + rhs * (k + 1)] = low
        if k < STEPS:
            both = jnp.concatenate([high, low], axis=0)
            vert[c, m, :, 0:unk] = both[:, 0:unk]
            vert[c, m + 2, :, unk:wide] = both[:, unk:wide]

    def borders(c):
        x, y = columns[c]
        return [("gx", 0, x == 0), ("gx", 1, x == nx - 1), ("gy", 0, y == 0), ("gy", 1, y == ny - 1)]

    def has(axis, side):
        here, count = (gx, n_gx) if axis == "gx" else (gy, n_gy)
        return here > 0 if side == 0 else here < count - 1

    def halo_copy(k, c, axis, side):
        x, y = columns[c]
        if axis == "gx":
            target, land, at, ss, rs = gx, rx, y, send_x, recv_x
        else:
            target, land, at, ss, rs = gy, ry, x, send_y, recv_y
        target = target - 1 if side == 0 else target + 1
        return pltpu.make_async_remote_copy(
            src_ref=tall.at[k, x, y], dst_ref=land.at[k, 1 - side, at],
            send_sem=ss.at[k, side, at], recv_sem=rs.at[k, 1 - side, at],
            device_id={axis: target}, device_id_type=MESH)

    def halo_wait(k, c, axis, side):
        x, y = columns[c]
        if axis == "gx":
            target, land, at, ss, rs = gx, rx, y, send_x, recv_x
        else:
            target, land, at, ss, rs = gy, ry, x, send_y, recv_y
        target = target - 1 if side == 0 else target + 1
        pltpu.make_async_remote_copy(
            src_ref=tall.at[k, x, y], dst_ref=land.at[k, side, at],
            send_sem=ss.at[k, side, at], recv_sem=rs.at[k, side, at],
            device_id={axis: target}, device_id_type=MESH).wait_recv()

    def send_column(k, c):
        for axis, side, edge in borders(c):
            if edge:
                @pl.when(has(axis, side))
                def _():
                    halo_copy(k, c, axis, side).start()

    start_copy.wait()
    for c, (x, y) in enumerate(columns):
        vert[c, 1, :, unk:wide] = jnp.zeros((2 * rhs, unk), BF16)
        vert[c, pairs, :, 0:unk] = jnp.zeros((2 * rhs, unk), BF16)
        for m in range(pairs):
            store_basis(0, c, m, jnp.concatenate([start_ref[x, y, 2 * m], start_ref[x, y, 2 * m + 1]], axis=1))
    for axis, land in (("gx", rx), ("gy", ry)):
        for side in (0, 1):
            @pl.when(jnp.logical_not(has(axis, side)))
            def _():
                for k in range(STEPS):
                    land[k, side] = jnp.zeros(land.shape[2:], F32)

    pl.semaphore_wait(barrier, n_gx + n_gy - 2)
    for c in range(len(columns)):
        send_column(0, c)

    def order(c):
        marks = [edge for _, _, edge in borders(c)]
        near = [d for d in range(4) if not marks[d]]
        far = [d for d in range(4) if marks[d]]
        return near, far

    zeros = jnp.zeros((unk, unk), F32)

    def prepare(c):
        near, far = order(c)

        def body(m, carry):
            low, up = raw.at[c, 2 * m], raw.at[c, 2 * m + 1]
            pieces = [
                ((low[0], low[6]), (up[5], up[0])),
                ((zeros, low[5]), (up[6], zeros)),
            ]
            for d in near + far:
                pieces.append(((low[1 + d], zeros), (zeros, up[1 + d])))
            for at, halves in enumerate(pieces):
                for half, (left, right) in enumerate(halves):
                    high, rest = limbs(jnp.concatenate([left, right], axis=1))
                    lanes = slice(at * wide, (at + 1) * wide)
                    weights[c, m, half * unk : (half + 1) * unk, lanes] = high
                    weights[c, m, wide + half * unk : wide + (half + 1) * unk, lanes] = rest
            return carry

        lax.fori_loop(0, pairs, body, 0)

    def fold(product):
        rows = product[0:rhs] + product[rhs : 2 * rhs]
        return rows[:, 0:wide] + rows[:, wide : 2 * wide]

    def rows_of(k, c, m):
        return jnp.concatenate(
            [limb[c, m, rhs * k : rhs * (k + 1)], limb[c, m, cols + rhs * k : cols + rhs * (k + 1)]], axis=0)

    def neighbour(c, d):
        x, y = columns[c]
        step = ((-1, 0), (1, 0), (0, -1), (0, 1))[d]
        return columns.index((x + step[0], y + step[1]))

    def near_part(k, c):
        near, _ = order(c)

        def body(i, carry):
            for s in range(chunk):
                m = i * chunk + s
                pieces = [rows_of(k, c, m), vert[c, m + 1]]
                pieces += [rows_of(k, neighbour(c, d), m) for d in near]
                left = jnp.concatenate(pieces, axis=1)
                partial[c, m] = fold(dot_nt(left, weights[c, m, :, 0 : left.shape[1]]))
            return carry

        lax.fori_loop(0, pairs // chunk, body, 0)

    def far_part(k, c):
        x, y = columns[c]
        near, far = order(c)
        for d in far:
            axis, side, _ = borders(c)[d]

            @pl.when(has(axis, side))
            def _():
                halo_wait(k, c, axis, side)

        def body(i, carry):
            for s in range(chunk):
                m = i * chunk + s
                pieces = []
                for d in far:
                    value = rx[k, d, y, m] if d < 2 else ry[k, d - 2, x, m]
                    pieces.append(jnp.concatenate(limbs(value), axis=0))
                applied = partial[c, m]
                if pieces:
                    left = jnp.concatenate(pieces, axis=1)
                    begin = (2 + len(near)) * wide
                    applied = applied + fold(dot_nt(left, weights[c, m, :, begin : begin + left.shape[1]]))
                current = tall[k, x, y, m]
                if k == 0:
                    following = (applied - 8.0 * current) * (1.0 / 6.0)
                else:
                    following = (applied - 8.0 * current) * (2.0 / 6.0) - tall[k - 1, x, y, m]
                store_basis(k + 1, c, m, following)
            return carry

        lax.fori_loop(0, pairs // chunk, body, 0)

    def gram_rows(k):
        count = rhs * (k + 1)
        total_high = jnp.zeros((2 * rhs, count), F32)
        total_low = jnp.zeros((2 * rhs, count), F32)
        for c in range(len(columns)):
            for m in range(0, pairs, 2):
                span = range(m, min(m + 2, pairs))
                left = jnp.concatenate([rows_of(k, c, q) for q in span], axis=1)
                high = jnp.concatenate([limb[c, q, 0:count] for q in span], axis=1)
                low = jnp.concatenate([limb[c, q, cols : cols + count] for q in span], axis=1)
                total_high += dot_nt(left, high)
                total_low += dot_nt(left, low)
        total = total_high + total_low
        total = total[0:rhs] + total[rhs : 2 * rhs]
        gram_x[k, gx] = jnp.concatenate([total, jnp.zeros((rhs, wide - count), F32)], axis=1)

    for c in range(len(columns)):
        raw_copy(c).wait()
        prepare(c)
    axes = {"gx": (gx, n_gx, gram_x, send_gx, recv_gx), "gy": (gy, n_gy, gram_y, send_gy, recv_gy)}

    def gram_copy(axis, k, d, receive=False):
        here, count, slots, send, recv = axes[axis]
        other = lax.rem(here + d, count)
        slot = other if receive else here
        return pltpu.make_async_remote_copy(
            src_ref=slots.at[k, slot], dst_ref=slots.at[k, slot], send_sem=send.at[k, d],
            recv_sem=recv.at[k, slot], device_id={axis: other}, device_id_type=MESH)

    def gram_send(axis, k):
        for d in range(1, axes[axis][1]):
            gram_copy(axis, k, d).start()

    def gram_sum(axis, k):
        _, count, slots, _, _ = axes[axis]
        for d in range(1, count):
            gram_copy(axis, k, d, receive=True).wait_recv()
        total = slots[k, 0]
        for i in range(1, count):
            total = total + slots[k, i]
        return total

    def gram_turn(k):
        gram_y[k, gy] = gram_sum("gx", k)
        gram_send("gy", k)

    for k in range(STEPS):
        gram_rows(k)
        gram_send("gx", k)
        for c in range(len(columns)):
            near_part(k, c)
        gram_turn(k)
        for c in range(len(columns)):
            far_part(k, c)
            if k + 1 < STEPS:
                send_column(k + 1, c)
    gram_rows(STEPS)
    gram_send("gx", STEPS)

    for c, (x, y) in enumerate(columns):
        def turn(i, carry):
            for s in range(chunk):
                m = i * chunk + s
                pieces = [tall[k, x, y, m] for k in range(STEPS + 1)]
                block = jnp.concatenate(pieces + [jnp.zeros((wide - cols, wide), F32)], axis=0).T
                turned[c, m] = jnp.concatenate(limbs(block), axis=1)
            return carry

        lax.fori_loop(0, pairs // chunk, turn, 0)

    front = STEPS * rhs
    rows = lax.broadcasted_iota(jnp.int32, (front, wide), 0)
    lane = lax.broadcasted_iota(jnp.int32, (front, wide), 1)
    lower = jnp.concatenate([gram_sum("gy", k) for k in range(STEPS)], axis=0)
    square = jnp.concatenate([lower, jnp.zeros((wide - front, wide), F32)], axis=0)
    whole = jnp.where(lane > rows, square.T[0:front], lower)
    on_diagonal = jnp.where(lane == rows, whole, 0.0)
    norm_rows = jnp.sqrt(jnp.sum(on_diagonal, axis=1, keepdims=True))
    norm_front = jnp.sqrt(jnp.sum(on_diagonal, axis=0, keepdims=True))
    line = lane[:1]
    whole = whole / (norm_rows * jnp.where(line < front, norm_front, 1.0))
    factored = [whole[8 * i : 8 * i + 8] for i in range(front // 8)]
    factored = eliminate(factored, 0, rhs)
    gram_turn(STEPS)
    factored = eliminate(factored, rhs, front)
    upper, inverse = split_factor(factored)
    inverse_full = jnp.concatenate([inverse, jnp.zeros((wide - front, wide), F32)], axis=0)

    last = gram_sum("gy", STEPS)
    last_rows = lax.broadcasted_iota(jnp.int32, (rhs, wide), 0)
    last_lane = lax.broadcasted_iota(jnp.int32, (rhs, wide), 1)
    on_diagonal = jnp.where(last_lane == last_rows + front, last, 0.0)
    norm_rows = jnp.sqrt(jnp.sum(on_diagonal, axis=1, keepdims=True))
    norm = norm_front + jnp.sqrt(jnp.sum(on_diagonal, axis=0, keepdims=True))
    norm = jnp.where(line < cols, norm, 1.0)
    last = last / (norm_rows * norm)
    side = dot_full(jnp.where(last_lane < front, last, 0.0), inverse_full, NT)
    rest = last[:, front:cols] - dot_full(side, side, NT)
    rest = jnp.concatenate([rest, jnp.zeros((rhs, wide - rhs), F32)], axis=1)
    rest = eliminate([rest[8 * i : 8 * i + 8] for i in range(rhs // 8)], 0, rhs)
    rest_upper, rest_inverse = split_factor(rest)
    below = dot_full(rest_inverse[:, 0:rhs], dot_full(side, inverse_full))

    def placed(value):
        return jnp.concatenate(
            [jnp.zeros((rhs, front), F32), value[:, 0:rhs], jnp.zeros((rhs, wide - cols), F32)], axis=1)

    beside = jnp.concatenate([jnp.zeros((front, wide), F32), side, jnp.zeros((wide - cols, wide), F32)], axis=0)
    triangle = jnp.concatenate([upper + beside.T[0:front], placed(rest_upper)], axis=0) * norm
    tri_ref[...] = triangle[:, 0:cols]
    inverse = jnp.concatenate(
        [inverse, placed(rest_inverse) - below, jnp.zeros((wide - cols, wide), F32)], axis=0) / norm
    inverse_high, inverse_low = limbs(inverse)
    right = jnp.concatenate(
        [jnp.concatenate([inverse_high, inverse_high], axis=1), jnp.concatenate([inverse_low, inverse_low], axis=1)],
        axis=0)

    def ortho_copy(c):
        x, y = columns[c]
        return pltpu.make_async_copy(ortho.at[c], ortho_hbm.at[x, y], ortho_sem.at[c])

    for c, (x, y) in enumerate(columns):
        def body(i, carry):
            for s in range(chunk):
                m = i * chunk + s
                product = dot_nt(turned[c, m], right)
                result = (product[:, 0:wide] + product[:, wide : 2 * wide])[:, 0:cols]
                ortho[c, 2 * m] = result[0:unk]
                ortho[c, 2 * m + 1] = result[unk:wide]
            return carry

        lax.fori_loop(0, pairs // chunk, body, 0)
        ortho_copy(c).start()

    for k in range(STEPS + 1):
        for axis in axes:
            for d in range(1, axes[axis][1]):
                gram_copy(axis, k, d).wait_send()
    for k in range(STEPS):
        for c in range(len(columns)):
            for axis, side, edge in borders(c):
                if edge:
                    @pl.when(has(axis, side))
                    def _():
                        halo_copy(k, c, axis, side).wait_send()
    for c in range(len(columns)):
        ortho_copy(c).wait()


def per_device(operator_blocks, start_block):
    nx, ny, nz, _, unk, _ = operator_blocks.shape
    rhs = start_block.shape[-1]
    n_gx, n_gy = lax.axis_size("gx"), lax.axis_size("gy")
    pairs, wide, cols, count = nz // 2, 2 * unk, (STEPS + 1) * rhs, nx * ny
    assert nz % 2 == 0 and wide == 128 and rhs % 16 == 0 and cols <= wide
    dma = pltpu.SemaphoreType.DMA
    return pl.pallas_call(
        functools.partial(kernel, (n_gx, n_gy, nx, ny, nz, unk, rhs)),
        out_shape=(
            jax.ShapeDtypeStruct((nx, ny, nz, unk, cols), F32),
            jax.ShapeDtypeStruct((cols, cols), F32),
        ),
        in_specs=[pl.BlockSpec(memory_space=pl.ANY), pl.BlockSpec(memory_space=pl.ANY)],
        out_specs=(pl.BlockSpec(memory_space=pl.ANY), pl.BlockSpec(memory_space=pltpu.VMEM)),
        scratch_shapes=[
            pltpu.VMEM((nx, ny, nz, rhs, unk), F32),
            pltpu.VMEM((count, nz, 7, unk, unk), F32),
            pltpu.VMEM((count, pairs, 2 * wide, 6 * wide), BF16),
            pltpu.VMEM((STEPS + 1, nx, ny, pairs, rhs, wide), F32),
            pltpu.VMEM((count, pairs, 2 * cols, wide), BF16),
            pltpu.VMEM((count, pairs + 2, 2 * rhs, wide), BF16),
            pltpu.VMEM((count, pairs, rhs, wide), F32),
            pltpu.VMEM((STEPS, 2, ny, pairs, rhs, wide), F32),
            pltpu.VMEM((STEPS, 2, nx, pairs, rhs, wide), F32),
            pltpu.VMEM((STEPS + 1, n_gx, rhs, wide), F32),
            pltpu.VMEM((STEPS + 1, n_gy, rhs, wide), F32),
            pltpu.VMEM((count, pairs, wide, 2 * wide), BF16),
            pltpu.VMEM((count, nz, unk, cols), F32),
            dma,
            dma((count,)),
            dma((count,)),
            dma((STEPS, 2, ny)),
            dma((STEPS, 2, ny)),
            dma((STEPS, 2, nx)),
            dma((STEPS, 2, nx)),
            dma((STEPS + 1, n_gx)),
            dma((STEPS + 1, n_gx)),
            dma((STEPS + 1, n_gy)),
            dma((STEPS + 1, n_gy)),
        ],
        compiler_params=pltpu.CompilerParams(
            collective_id=0, has_side_effects=True, vmem_limit_bytes=52 * 1024 * 1024
        ),
        cost_estimate=pl.CostEstimate(flops=6_000_000_000, bytes_accessed=16_000_000, transcendentals=0),
    )(operator_blocks, jnp.swapaxes(start_block, -1, -2))


def solution(mesh):
    in_specs = (P("gx", "gy", None, None, None, None), P("gx", "gy", None, None, None))
    out_specs = (P("gx", "gy", None, None, None), P())
    return jax.shard_map(
        per_device, mesh=mesh, in_specs=in_specs, out_specs=out_specs, check_vma=False
    )
```

```python
import functools

import jax
import jax.numpy as jnp
from jax import lax
from jax.experimental import pallas as pl
from jax.experimental.pallas import tpu as pltpu
from jax.sharding import PartitionSpec as P

STEPS = 4
F32 = jnp.float32
BF16 = jnp.bfloat16
NT = (((1,), (1,)), ((), ()))
MESH = pl.DeviceIdType.MESH


def limbs(value):
    high = value.astype(BF16)
    return high, (value - high.astype(F32)).astype(BF16)


def dot_nt(left, right):
    return lax.dot_general(left, right, NT, preferred_element_type=F32)


def chunk_of(count, most):
    return max(size for size in range(1, most + 1) if count % size == 0)


def dot_full(left, right, dims=(((1,), (0,)), ((), ()))):
    return lax.dot_general(left, right, dims, precision=lax.Precision.HIGHEST, preferred_element_type=F32)


def eliminate(blocks, start, stop):
    lane = lax.broadcasted_iota(jnp.int32, blocks[0].shape, 1)
    rows = lax.broadcasted_iota(jnp.int32, blocks[0].shape, 0)
    line = lane[:1]
    blocks = list(blocks)
    for j in range(start, stop, 2):
        first, inside = divmod(j, 8)
        row_0 = blocks[first][inside : inside + 1, :]
        row_1 = blocks[first][inside + 1 : inside + 2, :]
        a, b, c = row_0[:, j : j + 1], row_0[:, j + 1 : j + 2], row_1[:, j + 1 : j + 2]
        inverse = 1.0 / (a * c - b * b)
        unit_0 = jnp.where(line == j, 1.0, jnp.where(line == j + 1, 0.0, row_0))
        unit_1 = jnp.where(line == j + 1, 1.0, jnp.where(line == j, 0.0, row_1))
        scaled_0 = (c * unit_0 - b * unit_1) * inverse
        scaled_1 = (a * unit_1 - b * unit_0) * inverse
        ratio = b / a
        second = jnp.where(line == j, -ratio, row_1 - ratio * row_0)
        pair = jnp.logical_or(lane == j, lane == j + 1)
        for i in range(first, len(blocks)):
            block = blocks[i]
            kept = jnp.where(pair, 0.0, block)
            update = kept - block[:, j : j + 1] * scaled_0 - block[:, j + 1 : j + 2] * scaled_1
            if i == first:
                update = jnp.where(rows > inside + 1, update, jnp.where(rows == inside + 1, second, block))
            blocks[i] = update
    return blocks


def split_factor(blocks):
    factored = jnp.concatenate(blocks, axis=0)
    lane = lax.broadcasted_iota(jnp.int32, factored.shape, 1)
    rows = lax.broadcasted_iota(jnp.int32, factored.shape, 0)
    diagonal = jnp.sum(jnp.where(lane == rows, factored, 0.0), axis=1, keepdims=True)
    root = jnp.sqrt(diagonal)
    scale = 1.0 / root
    upper = jnp.where(lane > rows, factored * scale, jnp.where(lane == rows, root, 0.0))
    inverse = jnp.where(lane < rows, factored * scale, jnp.where(lane == rows, scale, 0.0))
    return upper, inverse


class Columns:
    def __init__(self, nx, ny):
        self.at = [(x, y) for x in range(nx) for y in range(ny)]
        self.nx, self.ny = nx, ny

    def borders(self, c):
        x, y = self.at[c]
        return [("gx", 0, x == 0), ("gx", 1, x == self.nx - 1), ("gy", 0, y == 0), ("gy", 1, y == self.ny - 1)]

    def order(self, c):
        marks = [edge for _, _, edge in self.borders(c)]
        return sorted(range(4), key=lambda d: marks[d])

    def neighbour(self, c, d):
        x, y = self.at[c]
        x, y = x + (-1, 1, 0, 0)[d], y + (0, 0, -1, 1)[d]
        return self.at.index((x, y)) if (x, y) in self.at else None


def repack_kernel(dims, blocks_hbm, weights, raw, raw_sem):
    nx, ny, nz, unk, rhs = dims
    columns = Columns(nx, ny)
    wide = 2 * unk

    def raw_copy(c):
        x, y = columns.at[c]
        return pltpu.make_async_copy(blocks_hbm.at[x, y], raw.at[c], raw_sem.at[c])

    for c in range(len(columns.at)):
        raw_copy(c).start()
    for c in range(len(columns.at)):
        raw_copy(c).wait()
        first, second, third, fourth = (1 + d for d in columns.order(c))
        zeros = jnp.zeros((unk, unk), F32)

        def body(m, carry):
            low, up = raw.at[c, 2 * m], raw.at[c, 2 * m + 1]
            halves = (
                ((low[0], low[6]), (low[first], low[5]), (low[third], low[fourth]), (low[second], zeros)),
                ((up[5], up[0]), (up[6], up[first]), (up[fourth], up[third]), (zeros, up[second])),
            )
            for half, pieces in enumerate(halves):
                for at, (left, right) in enumerate(pieces):
                    high, rest = limbs(jnp.concatenate([left, right], axis=1))
                    lanes = slice(at * wide, (at + 1) * wide)
                    weights[c, m, half, 0:unk, lanes] = high
                    weights[c, m, half, unk : 2 * unk, lanes] = rest
            return carry

        lax.fori_loop(0, nz // 2, body, 0)

def steps_kernel(dims, weights, start_ref, turned, gram_ref, tall, limb, mixed, partial, rx, ry, gram_x, gram_y,
                 send_x, recv_x, send_y, recv_y, send_gx, recv_gx, send_gy, recv_gy):
    n_gx, n_gy, nx, ny, nz, unk, rhs = dims
    pairs = nz // 2
    wide = 2 * unk
    cols = (STEPS + 1) * rhs
    gx, gy = lax.axis_index("gx"), lax.axis_index("gy")
    geometry = Columns(nx, ny)
    columns, borders, order, neighbour = geometry.at, geometry.borders, geometry.order, geometry.neighbour
    chunk = chunk_of(pairs, 6)

    barrier = pltpu.get_barrier_semaphore()
    for d in range(1, n_gx):
        pl.semaphore_signal(barrier, inc=1, device_id={"gx": lax.rem(gx + d, n_gx)}, device_id_type=MESH)
    for d in range(1, n_gy):
        pl.semaphore_signal(barrier, inc=1, device_id={"gy": lax.rem(gy + d, n_gy)}, device_id_type=MESH)

    def store_basis(k, c, m, value):
        x, y = columns[c]
        tall[k, x, y, m] = value
        high, low = limbs(value)
        limb[c, m, rhs * k : rhs * (k + 1)] = high
        limb[c, m, cols + rhs * k : cols + rhs * (k + 1)] = low
        if k < STEPS:
            both = jnp.concatenate([high, low], axis=0)
            mixed[c, m, 1, :, 0:unk] = both[:, 0:unk]
            mixed[c, m + 2, 0, :, unk:wide] = both[:, unk:wide]
            for user in range(len(columns)):
                if neighbour(user, order(user)[0]) == c:
                    mixed[user, m + 1, 0, :, 0:unk] = both[:, 0:unk]
                    mixed[user, m + 1, 1, :, unk:wide] = both[:, unk:wide]

    def has(axis, side):
        here, count = (gx, n_gx) if axis == "gx" else (gy, n_gy)
        return here > 0 if side == 0 else here < count - 1

    def halo_copy(k, c, axis, side):
        x, y = columns[c]
        if axis == "gx":
            target, land, at, ss, rs = gx, rx, y, send_x, recv_x
        else:
            target, land, at, ss, rs = gy, ry, x, send_y, recv_y
        target = target - 1 if side == 0 else target + 1
        return pltpu.make_async_remote_copy(
            src_ref=tall.at[k, x, y], dst_ref=land.at[k, 1 - side, at],
            send_sem=ss.at[k, side, at], recv_sem=rs.at[k, 1 - side, at],
            device_id={axis: target}, device_id_type=MESH)

    def halo_wait(k, c, axis, side):
        x, y = columns[c]
        if axis == "gx":
            target, land, at, ss, rs = gx, rx, y, send_x, recv_x
        else:
            target, land, at, ss, rs = gy, ry, x, send_y, recv_y
        target = target - 1 if side == 0 else target + 1
        pltpu.make_async_remote_copy(
            src_ref=tall.at[k, x, y], dst_ref=land.at[k, side, at],
            send_sem=ss.at[k, side, at], recv_sem=rs.at[k, side, at],
            device_id={axis: target}, device_id_type=MESH).wait_recv()

    def send_column(k, c):
        for axis, side, edge in borders(c):
            if edge:
                @pl.when(has(axis, side))
                def _():
                    halo_copy(k, c, axis, side).start()

    for c, (x, y) in enumerate(columns):
        mixed[c, 1, 0, :, unk:wide] = jnp.zeros((2 * rhs, unk), BF16)
        mixed[c, pairs, 1, :, 0:unk] = jnp.zeros((2 * rhs, unk), BF16)
        for m in range(pairs):
            store_basis(0, c, m, jnp.concatenate([start_ref[x, y, 2 * m], start_ref[x, y, 2 * m + 1]], axis=1))
    for axis, land in (("gx", rx), ("gy", ry)):
        for side in (0, 1):
            @pl.when(jnp.logical_not(has(axis, side)))
            def _():
                for k in range(STEPS):
                    land[k, side] = jnp.zeros(land.shape[2:], F32)

    pl.semaphore_wait(barrier, n_gx + n_gy - 2)
    for c in range(len(columns)):
        send_column(0, c)

    def apply_tile(c, m, tile, operands):
        results = []
        for half in range(2):
            product = dot_nt(weights[c, m, half, :, 2 * wide * tile : 2 * wide * (tile + 1)], operands[half])
            results.append(product[0:unk] + product[unk : 2 * unk])
        return jnp.concatenate(results, axis=0)

    def rows_of(k, c, m):
        return jnp.concatenate(
            [limb[c, m, rhs * k : rhs * (k + 1)], limb[c, m, cols + rhs * k : cols + rhs * (k + 1)]], axis=0)

    def wait_halos(k, c):
        for axis, side, edge in borders(c):
            if edge:
                @pl.when(has(axis, side))
                def _():
                    halo_wait(k, c, axis, side)

    def near_part(k, c):
        def body(i, carry):
            for s in range(chunk):
                m = i * chunk + s
                own = rows_of(k, c, m)
                operands = [jnp.concatenate([own, mixed[c, m + 1, half]], axis=1) for half in range(2)]
                partial[c, m] = apply_tile(c, m, 0, operands)
            return carry

        lax.fori_loop(0, pairs // chunk, body, 0)

    def far_part(k, c):
        x, y = columns[c]
        _, second, third, fourth = order(c)
        wait_halos(k, c)

        def values(d, m):
            other = neighbour(c, d)
            if other is None:
                return rx[k, d, y, m] if d < 2 else ry[k, d - 2, x, m]
            return tall[k, columns[other][0], columns[other][1], m]

        def body(i, carry):
            in_low = lax.broadcasted_iota(jnp.int32, (rhs, wide), 1) < unk
            for s in range(chunk):
                m = i * chunk + s
                if neighbour(c, second) is None:
                    alone = jnp.concatenate(limbs(values(second, m)), axis=0)
                else:
                    alone = rows_of(k, neighbour(c, second), m)
                plain, rolled = values(third, m), pltpu.roll(values(fourth, m), unk, 1)
                pairs_of = (jnp.where(in_low, plain, rolled), jnp.where(in_low, rolled, plain))
                operands = [
                    jnp.concatenate([jnp.concatenate(limbs(both), axis=0), alone], axis=1) for both in pairs_of]
                applied = (partial[c, m] + apply_tile(c, m, 1, operands)).T
                applied = applied[0:rhs] + applied[rhs : 2 * rhs]
                current = tall[k, x, y, m]
                if k == 0:
                    following = (applied - 8.0 * current) * (1.0 / 6.0)
                else:
                    following = (applied - 8.0 * current) * (2.0 / 6.0) - tall[k - 1, x, y, m]
                store_basis(k + 1, c, m, following)
            return carry

        lax.fori_loop(0, pairs // chunk, body, 0)

    def gram_rows(k):
        count = rhs * (k + 1)
        total_high = jnp.zeros((2 * rhs, count), F32)
        total_low = jnp.zeros((2 * rhs, count), F32)
        for c in range(len(columns)):
            for m in range(0, pairs, 2):
                span = range(m, min(m + 2, pairs))
                left = jnp.concatenate([rows_of(k, c, q) for q in span], axis=1)
                high = jnp.concatenate([limb[c, q, 0:count] for q in span], axis=1)
                low = jnp.concatenate([limb[c, q, cols : cols + count] for q in span], axis=1)
                total_high += dot_nt(left, high)
                total_low += dot_nt(left, low)
        total = total_high + total_low
        total = total[0:rhs] + total[rhs : 2 * rhs]
        gram_x[k, gx] = jnp.concatenate([total, jnp.zeros((rhs, wide - count), F32)], axis=1)

    axes = {"gx": (gx, n_gx, gram_x, send_gx, recv_gx), "gy": (gy, n_gy, gram_y, send_gy, recv_gy)}

    def gram_copy(axis, k, d, receive=False):
        here, count, slots, send, recv = axes[axis]
        other = lax.rem(here + d, count)
        slot = other if receive else here
        return pltpu.make_async_remote_copy(
            src_ref=slots.at[k, slot], dst_ref=slots.at[k, slot], send_sem=send.at[k, d],
            recv_sem=recv.at[k, slot], device_id={axis: other}, device_id_type=MESH)

    def gram_send(axis, k):
        for d in range(1, axes[axis][1]):
            gram_copy(axis, k, d).start()

    def gram_sum(axis, k):
        _, count, slots, _, _ = axes[axis]
        for d in range(1, count):
            gram_copy(axis, k, d, receive=True).wait_recv()
        total = slots[k, 0]
        for i in range(1, count):
            total = total + slots[k, i]
        return total

    def gram_turn(k):
        gram_y[k, gy] = gram_sum("gx", k)
        gram_send("gy", k)

    for k in range(STEPS):
        gram_rows(k)
        gram_send("gx", k)
        for c in range(len(columns)):
            near_part(k, c)
        gram_turn(k)
        for c in range(len(columns)):
            far_part(k, c)
            if k + 1 < STEPS:
                send_column(k + 1, c)
    gram_rows(STEPS)
    gram_send("gx", STEPS)

    for c, (x, y) in enumerate(columns):
        def turn(i, carry):
            for s in range(chunk):
                m = i * chunk + s
                pieces = [tall[k, x, y, m] for k in range(STEPS + 1)]
                block = jnp.concatenate(pieces + [jnp.zeros((wide - cols, wide), F32)], axis=0).T
                turned[c, m] = jnp.concatenate(limbs(block), axis=1)
            return carry

        lax.fori_loop(0, pairs // chunk, turn, 0)

    gram_turn(STEPS)
    for k in range(STEPS + 1):
        gram_ref[k] = gram_sum("gy", k)

    for k in range(STEPS + 1):
        for axis in axes:
            for d in range(1, axes[axis][1]):
                gram_copy(axis, k, d).wait_send()
    for k in range(STEPS):
        for c in range(len(columns)):
            for axis, side, edge in borders(c):
                if edge:
                    @pl.when(has(axis, side))
                    def _():
                        halo_copy(k, c, axis, side).wait_send()


def factor_kernel(dims, turned, gram_ref, ortho_hbm, tri_ref, ortho, ortho_sem):
    nx, ny, nz, unk, rhs = dims
    columns = Columns(nx, ny).at
    pairs, wide, cols = nz // 2, 2 * unk, (STEPS + 1) * rhs
    chunk = chunk_of(pairs, 6)

    front = STEPS * rhs
    rows = lax.broadcasted_iota(jnp.int32, (front, wide), 0)
    lane = lax.broadcasted_iota(jnp.int32, (front, wide), 1)
    lower = jnp.concatenate([gram_ref[k] for k in range(STEPS)], axis=0)
    square = jnp.concatenate([lower, jnp.zeros((wide - front, wide), F32)], axis=0)
    whole = jnp.where(lane > rows, square.T[0:front], lower)
    on_diagonal = jnp.where(lane == rows, whole, 0.0)
    norm_rows = jnp.sqrt(jnp.sum(on_diagonal, axis=1, keepdims=True))
    norm_front = jnp.sqrt(jnp.sum(on_diagonal, axis=0, keepdims=True))
    line = lane[:1]
    whole = whole / (norm_rows * jnp.where(line < front, norm_front, 1.0))
    factored = [whole[8 * i : 8 * i + 8] for i in range(front // 8)]
    factored = eliminate(factored, 0, front)
    upper, inverse = split_factor(factored)
    inverse_full = jnp.concatenate([inverse, jnp.zeros((wide - front, wide), F32)], axis=0)

    last = gram_ref[STEPS]
    last_rows = lax.broadcasted_iota(jnp.int32, (rhs, wide), 0)
    last_lane = lax.broadcasted_iota(jnp.int32, (rhs, wide), 1)
    on_diagonal = jnp.where(last_lane == last_rows + front, last, 0.0)
    norm_rows = jnp.sqrt(jnp.sum(on_diagonal, axis=1, keepdims=True))
    norm = norm_front + jnp.sqrt(jnp.sum(on_diagonal, axis=0, keepdims=True))
    norm = jnp.where(line < cols, norm, 1.0)
    last = last / (norm_rows * norm)
    side = dot_full(jnp.where(last_lane < front, last, 0.0), inverse_full, NT)
    rest = last[:, front:cols] - dot_full(side, side, NT)
    rest = jnp.concatenate([rest, jnp.zeros((rhs, wide - rhs), F32)], axis=1)
    rest = eliminate([rest[8 * i : 8 * i + 8] for i in range(rhs // 8)], 0, rhs)
    rest_upper, rest_inverse = split_factor(rest)
    below = dot_full(rest_inverse[:, 0:rhs], dot_full(side, inverse_full))

    def placed(value):
        return jnp.concatenate(
            [jnp.zeros((rhs, front), F32), value[:, 0:rhs], jnp.zeros((rhs, wide - cols), F32)], axis=1)

    beside = jnp.concatenate([jnp.zeros((front, wide), F32), side, jnp.zeros((wide - cols, wide), F32)], axis=0)
    triangle = jnp.concatenate([upper + beside.T[0:front], placed(rest_upper)], axis=0) * norm
    tri_ref[...] = triangle[:, 0:cols]
    inverse = jnp.concatenate(
        [inverse, placed(rest_inverse) - below, jnp.zeros((wide - cols, wide), F32)], axis=0) / norm
    inverse_high, inverse_low = limbs(inverse)
    right = jnp.concatenate(
        [jnp.concatenate([inverse_high, inverse_high], axis=1), jnp.concatenate([inverse_low, inverse_low], axis=1)],
        axis=0)

    def ortho_copy(c):
        x, y = columns[c]
        return pltpu.make_async_copy(ortho.at[c], ortho_hbm.at[x, y], ortho_sem.at[c])

    for c, (x, y) in enumerate(columns):
        def body(i, carry):
            for s in range(chunk):
                m = i * chunk + s
                product = dot_nt(turned[c, m], right)
                result = (product[:, 0:wide] + product[:, wide : 2 * wide])[:, 0:cols]
                ortho[c, 2 * m] = result[0:unk]
                ortho[c, 2 * m + 1] = result[unk:wide]
            return carry

        lax.fori_loop(0, pairs // chunk, body, 0)
        ortho_copy(c).start()

    for c in range(len(columns)):
        ortho_copy(c).wait()


def per_device(operator_blocks, start_block):
    nx, ny, nz, _, unk, _ = operator_blocks.shape
    rhs = start_block.shape[-1]
    n_gx, n_gy = lax.axis_size("gx"), lax.axis_size("gy")
    pairs, wide, cols, count = nz // 2, 2 * unk, (STEPS + 1) * rhs, nx * ny
    assert count > 1 and nz % 2 == 0 and wide == 128 and rhs % 16 == 0 and cols <= wide
    dma = pltpu.SemaphoreType.DMA
    vmem, anywhere = pl.BlockSpec(memory_space=pltpu.VMEM), pl.BlockSpec(memory_space=pl.ANY)
    limit = 24 * 1024 * 1024
    local = (nx, ny, nz, unk, rhs)
    weights = pl.pallas_call(
        functools.partial(repack_kernel, local),
        out_shape=jax.ShapeDtypeStruct((count, pairs, 2, 2 * unk, 4 * wide), BF16),
        in_specs=[anywhere],
        out_specs=vmem,
        scratch_shapes=[pltpu.VMEM((count, nz, 7, unk, unk), F32), dma((count,))],
        compiler_params=pltpu.CompilerParams(vmem_limit_bytes=52 * 1024 * 1024),
        cost_estimate=pl.CostEstimate(flops=10_000_000, bytes_accessed=16_000_000, transcendentals=0),
    )(operator_blocks)
    turned, gram = pl.pallas_call(
        functools.partial(steps_kernel, (n_gx, n_gy, nx, ny, nz, unk, rhs)),
        out_shape=(
            jax.ShapeDtypeStruct((count, pairs, wide, 2 * wide), BF16),
            jax.ShapeDtypeStruct((STEPS + 1, rhs, wide), F32),
        ),
        in_specs=[vmem, vmem],
        out_specs=(vmem, vmem),
        scratch_shapes=[
            pltpu.VMEM((STEPS + 1, nx, ny, pairs, rhs, wide), F32),
            pltpu.VMEM((count, pairs, 2 * cols, wide), BF16),
            pltpu.VMEM((count, pairs + 2, 2, 2 * rhs, wide), BF16),
            pltpu.VMEM((count, pairs, wide, 2 * rhs), F32),
            pltpu.VMEM((STEPS, 2, ny, pairs, rhs, wide), F32),
            pltpu.VMEM((STEPS, 2, nx, pairs, rhs, wide), F32),
            pltpu.VMEM((STEPS + 1, n_gx, rhs, wide), F32),
            pltpu.VMEM((STEPS + 1, n_gy, rhs, wide), F32),
            dma((STEPS, 2, ny)),
            dma((STEPS, 2, ny)),
            dma((STEPS, 2, nx)),
            dma((STEPS, 2, nx)),
            dma((STEPS + 1, n_gx)),
            dma((STEPS + 1, n_gx)),
            dma((STEPS + 1, n_gy)),
            dma((STEPS + 1, n_gy)),
        ],
        compiler_params=pltpu.CompilerParams(collective_id=0, has_side_effects=True, vmem_limit_bytes=limit),
        cost_estimate=pl.CostEstimate(flops=6_000_000_000, bytes_accessed=16_000_000, transcendentals=0),
    )(weights, jnp.swapaxes(start_block, -1, -2))
    return pl.pallas_call(
        functools.partial(factor_kernel, local),
        out_shape=(
            jax.ShapeDtypeStruct((nx, ny, nz, unk, cols), F32),
            jax.ShapeDtypeStruct((cols, cols), F32),
        ),
        in_specs=[vmem, vmem],
        out_specs=(anywhere, vmem),
        scratch_shapes=[pltpu.VMEM((count, nz, unk, cols), F32), dma((count,))],
        compiler_params=pltpu.CompilerParams(vmem_limit_bytes=limit),
        cost_estimate=pl.CostEstimate(flops=400_000_000, bytes_accessed=4_000_000, transcendentals=0),
    )(turned, gram)


def solution(mesh):
    in_specs = (P("gx", "gy", None, None, None, None), P("gx", "gy", None, None, None))
    out_specs = (P("gx", "gy", None, None, None), P())
    return jax.shard_map(
        per_device, mesh=mesh, in_specs=in_specs, out_specs=out_specs, check_vma=False
    )
```

```python
import functools

import jax
import jax.numpy as jnp
from jax import lax
from jax.experimental import pallas as pl
from jax.experimental.pallas import tpu as pltpu
from jax.sharding import PartitionSpec as P

STEPS = 4
F32 = jnp.float32
BF16 = jnp.bfloat16
NT = (((1,), (1,)), ((), ()))
MESH = pl.DeviceIdType.MESH


def limbs(value):
    high = value.astype(BF16)
    return high, (value - high.astype(F32)).astype(BF16)


def dot_nt(left, right):
    return lax.dot_general(left, right, NT, preferred_element_type=F32)


def chunk_of(count, most):
    return max(size for size in range(1, most + 1) if count % size == 0)


def dot_full(left, right, dims=(((1,), (0,)), ((), ()))):
    return lax.dot_general(left, right, dims, precision=lax.Precision.HIGHEST, preferred_element_type=F32)


def eliminate(blocks, start, stop):
    lane = lax.broadcasted_iota(jnp.int32, blocks[0].shape, 1)
    rows = lax.broadcasted_iota(jnp.int32, blocks[0].shape, 0)
    line = lane[:1]
    for j in range(start, stop, 2):
        first, inside = divmod(j, 8)
        row_0 = blocks[first][inside : inside + 1, :]
        row_1 = blocks[first][inside + 1 : inside + 2, :]
        a, b, c = row_0[:, j : j + 1], row_0[:, j + 1 : j + 2], row_1[:, j + 1 : j + 2]
        inverse = 1.0 / (a * c - b * b)
        unit_0 = jnp.where(line == j, 1.0, jnp.where(line == j + 1, 0.0, row_0))
        unit_1 = jnp.where(line == j + 1, 1.0, jnp.where(line == j, 0.0, row_1))
        scaled_0 = (c * unit_0 - b * unit_1) * inverse
        scaled_1 = (a * unit_1 - b * unit_0) * inverse
        ratio = b / a
        second = jnp.where(line == j, -ratio, row_1 - ratio * row_0)
        pair = jnp.logical_or(lane == j, lane == j + 1)
        for i in range(first, len(blocks)):
            block = blocks[i]
            kept = jnp.where(pair, 0.0, block)
            update = kept - block[:, j : j + 1] * scaled_0 - block[:, j + 1 : j + 2] * scaled_1
            if i == first:
                update = jnp.where(rows > inside + 1, update, jnp.where(rows == inside + 1, second, block))
            blocks[i] = update
        yield


def split_factor(blocks):
    factored = jnp.concatenate(blocks, axis=0)
    lane = lax.broadcasted_iota(jnp.int32, factored.shape, 1)
    rows = lax.broadcasted_iota(jnp.int32, factored.shape, 0)
    diagonal = jnp.sum(jnp.where(lane == rows, factored, 0.0), axis=1, keepdims=True)
    root = jnp.sqrt(diagonal)
    scale = 1.0 / root
    upper = jnp.where(lane > rows, factored * scale, jnp.where(lane == rows, root, 0.0))
    inverse = jnp.where(lane < rows, factored * scale, jnp.where(lane == rows, scale, 0.0))
    return upper, inverse


def kernel(dims, blocks_hbm, start_ref, turned, right_ref, tri_ref, raw, weights, tall, limb, mixed,
           partial, rx, ry, gram_x, gram_y, raw_sem, send_x, recv_x, send_y, recv_y, send_gx, recv_gx,
           send_gy, recv_gy):
    n_gx, n_gy, nx, ny, nz, unk, rhs = dims
    pairs = nz // 2
    wide = 2 * unk
    cols = (STEPS + 1) * rhs
    gx, gy = lax.axis_index("gx"), lax.axis_index("gy")
    columns = [(x, y) for x in range(nx) for y in range(ny)]
    chunk = chunk_of(pairs, 6)

    def raw_copy(c):
        x, y = columns[c]
        return pltpu.make_async_copy(blocks_hbm.at[x, y], raw.at[c], raw_sem.at[c])

    for c in range(len(columns)):
        raw_copy(c).start()

    barrier = pltpu.get_barrier_semaphore()
    for d in range(1, n_gx):
        pl.semaphore_signal(barrier, inc=1, device_id={"gx": lax.rem(gx + d, n_gx)}, device_id_type=MESH)
    for d in range(1, n_gy):
        pl.semaphore_signal(barrier, inc=1, device_id={"gy": lax.rem(gy + d, n_gy)}, device_id_type=MESH)

    def borders(c):
        x, y = columns[c]
        return [("gx", 0, x == 0), ("gx", 1, x == nx - 1), ("gy", 0, y == 0), ("gy", 1, y == ny - 1)]

    def order(c):
        marks = [edge for _, _, edge in borders(c)]
        return sorted(range(4), key=lambda d: marks[d])

    def neighbour(c, d):
        x, y = columns[c]
        x, y = x + (-1, 1, 0, 0)[d], y + (0, 0, -1, 1)[d]
        return columns.index((x, y)) if (x, y) in columns else None

    def store_basis(k, c, m, value):
        x, y = columns[c]
        tall[k, x, y, m] = value
        high, low = limbs(value)
        limb[c, m, rhs * k : rhs * (k + 1)] = high
        limb[c, m, cols + rhs * k : cols + rhs * (k + 1)] = low
        if k < STEPS:
            both = jnp.concatenate([high, low], axis=0)
            mixed[c, m, 1, :, 0:unk] = both[:, 0:unk]
            mixed[c, m + 2, 0, :, unk:wide] = both[:, unk:wide]
            for user in range(len(columns)):
                if neighbour(user, order(user)[0]) == c:
                    mixed[user, m + 1, 0, :, 0:unk] = both[:, 0:unk]
                    mixed[user, m + 1, 1, :, unk:wide] = both[:, unk:wide]

    def has(axis, side):
        here, count = (gx, n_gx) if axis == "gx" else (gy, n_gy)
        return here > 0 if side == 0 else here < count - 1

    def halo_copy(k, c, axis, side):
        x, y = columns[c]
        if axis == "gx":
            target, land, at, ss, rs = gx, rx, y, send_x, recv_x
        else:
            target, land, at, ss, rs = gy, ry, x, send_y, recv_y
        target = target - 1 if side == 0 else target + 1
        return pltpu.make_async_remote_copy(
            src_ref=tall.at[k, x, y], dst_ref=land.at[k, 1 - side, at],
            send_sem=ss.at[k, side, at], recv_sem=rs.at[k, 1 - side, at],
            device_id={axis: target}, device_id_type=MESH)

    def halo_wait(k, c, axis, side):
        x, y = columns[c]
        if axis == "gx":
            target, land, at, ss, rs = gx, rx, y, send_x, recv_x
        else:
            target, land, at, ss, rs = gy, ry, x, send_y, recv_y
        target = target - 1 if side == 0 else target + 1
        pltpu.make_async_remote_copy(
            src_ref=tall.at[k, x, y], dst_ref=land.at[k, side, at],
            send_sem=ss.at[k, side, at], recv_sem=rs.at[k, side, at],
            device_id={axis: target}, device_id_type=MESH).wait_recv()

    def send_column(k, c):
        for axis, side, edge in borders(c):
            if edge:
                @pl.when(has(axis, side))
                def _():
                    halo_copy(k, c, axis, side).start()

    for c, (x, y) in enumerate(columns):
        mixed[c, 1, 0, :, unk:wide] = jnp.zeros((2 * rhs, unk), BF16)
        mixed[c, pairs, 1, :, 0:unk] = jnp.zeros((2 * rhs, unk), BF16)
        for m in range(pairs):
            store_basis(0, c, m, jnp.concatenate([start_ref[x, y, 2 * m], start_ref[x, y, 2 * m + 1]], axis=1))
    for axis, land in (("gx", rx), ("gy", ry)):
        for side in (0, 1):
            @pl.when(jnp.logical_not(has(axis, side)))
            def _():
                for k in range(STEPS):
                    land[k, side] = jnp.zeros(land.shape[2:], F32)

    pl.semaphore_wait(barrier, n_gx + n_gy - 2)
    for c in range(len(columns)):
        send_column(0, c)

    def prepare(c):
        first, second, third, fourth = (1 + d for d in order(c))
        zeros = jnp.zeros((unk, unk), F32)

        for m in range(pairs):
            low, up = raw.at[c, 2 * m], raw.at[c, 2 * m + 1]
            halves = (
                ((low[0], low[6]), (low[first], low[5]), (low[third], low[fourth]), (low[second], zeros)),
                ((up[5], up[0]), (up[6], up[first]), (up[fourth], up[third]), (zeros, up[second])),
            )
            for half, pieces in enumerate(halves):
                for at, (left, right) in enumerate(pieces):
                    high, rest = limbs(jnp.concatenate([left, right], axis=1))
                    lanes = slice(at * wide, (at + 1) * wide)
                    weights[c, m, half, 0:unk, lanes] = high
                    weights[c, m, half, unk : 2 * unk, lanes] = rest

    def apply_tile(c, m, tile, operands):
        results = []
        for half in range(2):
            product = dot_nt(weights[c, m, half, :, 2 * wide * tile : 2 * wide * (tile + 1)], operands[half])
            results.append(product[0:unk] + product[unk : 2 * unk])
        return jnp.concatenate(results, axis=0)

    def rows_of(k, c, m):
        return jnp.concatenate(
            [limb[c, m, rhs * k : rhs * (k + 1)], limb[c, m, cols + rhs * k : cols + rhs * (k + 1)]], axis=0)

    def wait_halos(k, c):
        for axis, side, edge in borders(c):
            if edge:
                @pl.when(has(axis, side))
                def _():
                    halo_wait(k, c, axis, side)

    def near_part(k, c, beside=iter(())):
        for m in range(pairs):
            own = rows_of(k, c, m)
            operands = [jnp.concatenate([own, mixed[c, m + 1, half]], axis=1) for half in range(2)]
            partial[c, m] = apply_tile(c, m, 0, operands)
            next(beside, None)

    def far_part(k, c):
        x, y = columns[c]
        _, second, third, fourth = order(c)
        wait_halos(k, c)

        def values(d, m):
            other = neighbour(c, d)
            if other is None:
                return rx[k, d, y, m] if d < 2 else ry[k, d - 2, x, m]
            return tall[k, columns[other][0], columns[other][1], m]

        def body(i, carry):
            in_low = lax.broadcasted_iota(jnp.int32, (rhs, wide), 1) < unk
            for s in range(chunk):
                m = i * chunk + s
                if neighbour(c, second) is None:
                    alone = jnp.concatenate(limbs(values(second, m)), axis=0)
                else:
                    alone = rows_of(k, neighbour(c, second), m)
                plain, rolled = values(third, m), pltpu.roll(values(fourth, m), unk, 1)
                pairs_of = (jnp.where(in_low, plain, rolled), jnp.where(in_low, rolled, plain))
                operands = [
                    jnp.concatenate([jnp.concatenate(limbs(both), axis=0), alone], axis=1) for both in pairs_of]
                applied = (partial[c, m] + apply_tile(c, m, 1, operands)).T
                applied = applied[0:rhs] + applied[rhs : 2 * rhs]
                current = tall[k, x, y, m]
                if k == 0:
                    following = (applied - 8.0 * current) * (1.0 / 6.0)
                else:
                    following = (applied - 8.0 * current) * (2.0 / 6.0) - tall[k - 1, x, y, m]
                store_basis(k + 1, c, m, following)
            return carry

        lax.fori_loop(0, pairs // chunk, body, 0)

    def gram_rows(k):
        count = rhs * (k + 1)
        total_high = jnp.zeros((2 * rhs, count), F32)
        total_low = jnp.zeros((2 * rhs, count), F32)
        for c in range(len(columns)):
            for m in range(0, pairs, 2):
                span = range(m, min(m + 2, pairs))
                left = jnp.concatenate([rows_of(k, c, q) for q in span], axis=1)
                high = jnp.concatenate([limb[c, q, 0:count] for q in span], axis=1)
                low = jnp.concatenate([limb[c, q, cols : cols + count] for q in span], axis=1)
                total_high += dot_nt(left, high)
                total_low += dot_nt(left, low)
        total = total_high + total_low
        total = total[0:rhs] + total[rhs : 2 * rhs]
        return total

    axes = {"gx": (gx, n_gx, gram_x, send_gx, recv_gx), "gy": (gy, n_gy, gram_y, send_gy, recv_gy)}
    early = STEPS - 1
    assert rhs * early * (early + 1) // 2 <= wide

    def put_gram(part, values):
        values = list(values)
        used = sum(value.shape[1] for value in values)
        if used < wide:
            values.append(jnp.zeros((rhs, wide - used), F32))
        gram_x[part, gx] = jnp.concatenate(values, axis=1)

    def gram_copy(axis, k, d, receive=False):
        here, count, slots, send, recv = axes[axis]
        other = lax.rem(here + d, count)
        slot = other if receive else here
        return pltpu.make_async_remote_copy(
            src_ref=slots.at[k, slot], dst_ref=slots.at[k, slot], send_sem=send.at[k, d],
            recv_sem=recv.at[k, slot], device_id={axis: other}, device_id_type=MESH)

    def gram_send(axis, k):
        for d in range(1, axes[axis][1]):
            gram_copy(axis, k, d).start()

    def gram_sum(axis, k):
        _, count, slots, _, _ = axes[axis]
        for d in range(1, count):
            gram_copy(axis, k, d, receive=True).wait_recv()
        total = slots[k, 0]
        for i in range(1, count):
            total = total + slots[k, i]
        return total

    def gram_turn(k):
        gram_y[k, gy] = gram_sum("gx", k)
        gram_send("gy", k)

    def lanes_from(value, begin, count):
        return jnp.concatenate([value[:, begin : begin + count], jnp.zeros((rhs, wide - count), F32)], axis=1)

    def append(known, norm, rows_value, at):
        rows = lax.broadcasted_iota(jnp.int32, (rhs, wide), 0)
        lane = lax.broadcasted_iota(jnp.int32, (rhs, wide), 1)
        on_diagonal = jnp.where(lane == rows + at, rows_value, 0.0)
        norm_rows = jnp.sqrt(jnp.sum(on_diagonal, axis=1, keepdims=True))
        norm = jnp.where(line // rhs == at // rhs, jnp.sqrt(jnp.sum(on_diagonal, axis=0, keepdims=True)), norm)
        scaled = rows_value / (norm_rows * norm)
        full = jnp.concatenate([known, jnp.zeros((wide - at, wide), F32)], axis=0)
        side = dot_full(jnp.where(lane < at, scaled, 0.0), full, NT)
        rest = scaled[:, at : at + rhs] - dot_full(side, side, NT)
        rest = lanes_from(rest, 0, rhs)
        rest = [rest[8 * i : 8 * i + 8] for i in range(rhs // 8)]
        for _ in eliminate(rest, 0, rhs):
            pass
        upper, inverse = split_factor(rest)
        below = dot_full(inverse[:, 0:rhs], dot_full(side, full))

        def placed(value):
            pieces = [jnp.zeros((rhs, at), F32), value[:, 0:rhs], jnp.zeros((rhs, wide - at - rhs), F32)]
            return jnp.concatenate([piece for piece in pieces if piece.shape[1]], axis=1)

        known = jnp.concatenate([known, placed(inverse) - below], axis=0)
        beside = jnp.concatenate(
            [jnp.zeros((at, wide), F32), side, jnp.zeros((wide - at - rhs, wide), F32)], axis=0).T
        return known, norm, placed(upper), beside[0:at]

    front = early * rhs
    rows = lax.broadcasted_iota(jnp.int32, (front, wide), 0)
    lane = lax.broadcasted_iota(jnp.int32, (front, wide), 1)
    line = lane[:1]

    def first_rows():
        total = gram_sum("gy", 0)
        pieces, begin = [], 0
        for k in range(early):
            pieces.append(lanes_from(total, begin, rhs * (k + 1)))
            begin += rhs * (k + 1)
        lower = jnp.concatenate(pieces, axis=0)
        square = jnp.concatenate([lower, jnp.zeros((wide - front, wide), F32)], axis=0)
        whole = jnp.where(lane > rows, square.T[0:front], lower)
        on_diagonal = jnp.where(lane == rows, whole, 0.0)
        norm_rows = jnp.sqrt(jnp.sum(on_diagonal, axis=1, keepdims=True))
        norm = jnp.where(line < front, jnp.sqrt(jnp.sum(on_diagonal, axis=0, keepdims=True)), 1.0)
        whole = whole / (norm_rows * norm)
        return [whole[8 * i : 8 * i + 8] for i in range(front // 8)], norm

    products = [gram_rows(0)]
    for c in range(len(columns)):
        raw_copy(c).wait()
        prepare(c)
        near_part(0, c)
    for k in range(STEPS):
        pivots = iter(())
        if k > 0:
            products.append(gram_rows(k))
        if k == early - 1:
            put_gram(0, products)
            gram_send("gx", 0)
        if k == early:
            put_gram(1, products[early:])
            gram_send("gx", 1)
            blocks, norm = first_rows()
            pivots = eliminate(blocks, 0, front)
        if k > 0:
            for c in range(len(columns)):
                near_part(k, c, pivots)
        for _ in pivots:
            pass
        if k == early - 1:
            gram_turn(0)
        for c in range(len(columns)):
            far_part(k, c)
            if k + 1 < STEPS:
                send_column(k + 1, c)
    gram_turn(1)
    put_gram(2, [gram_rows(STEPS)])
    gram_send("gx", 2)

    for c, (x, y) in enumerate(columns):
        for m in range(pairs):
            pieces = [tall[k, x, y, m] for k in range(STEPS + 1)]
            block = jnp.concatenate(pieces + [jnp.zeros((wide - cols, wide), F32)], axis=0).T
            turned[c, m] = jnp.concatenate(limbs(block), axis=1)

    upper, known = split_factor(blocks)
    fourth_rows = gram_sum("gy", 1)
    gram_turn(2)
    known, norm, upper_3, beside_3 = append(known, norm, fourth_rows, front)
    known, norm, upper_4, beside_4 = append(known, norm, gram_sum("gy", 2), front + rhs)
    triangle = jnp.concatenate([upper + beside_3, upper_3], axis=0) + beside_4
    triangle = jnp.concatenate([triangle, upper_4], axis=0) * norm
    tri_ref[...] = triangle
    inverse = jnp.concatenate([known, jnp.zeros((wide - cols, wide), F32)], axis=0) / norm
    high, low = limbs(inverse)
    right_ref[0:wide, 0:wide] = high
    right_ref[0:wide, wide : 2 * wide] = high
    right_ref[wide : 2 * wide, 0:wide] = low
    right_ref[wide : 2 * wide, wide : 2 * wide] = low

    for k in range(3):
        for axis in axes:
            for d in range(1, axes[axis][1]):
                gram_copy(axis, k, d).wait_send()
    for k in range(STEPS):
        for c in range(len(columns)):
            for axis, side, edge in borders(c):
                if edge:
                    @pl.when(has(axis, side))
                    def _():
                        halo_copy(k, c, axis, side).wait_send()


def product_kernel(dims, turned, right_ref, tri_in, ortho_hbm, tri_ref, ortho, ortho_sem):
    nx, ny, nz, unk, cols = dims
    wide = 2 * unk
    columns = [(x, y) for x in range(nx) for y in range(ny)]
    tri_ref[...] = tri_in[:, 0:cols]

    def ortho_copy(c):
        x, y = columns[c]
        return pltpu.make_async_copy(ortho.at[c], ortho_hbm.at[x, y], ortho_sem.at[c])

    for c in range(len(columns)):
        for m in range(nz // 2):
            product = dot_nt(turned[c, m], right_ref[...])
            result = (product[:, 0:wide] + product[:, wide : 2 * wide])[:, 0:cols]
            ortho[c, 2 * m] = result[0:unk]
            ortho[c, 2 * m + 1] = result[unk:wide]
        ortho_copy(c).start()
    for c in range(len(columns)):
        ortho_copy(c).wait()


def per_device(operator_blocks, start_block):
    nx, ny, nz, _, unk, _ = operator_blocks.shape
    rhs = start_block.shape[-1]
    n_gx, n_gy = lax.axis_size("gx"), lax.axis_size("gy")
    pairs, wide, cols, count = nz // 2, 2 * unk, (STEPS + 1) * rhs, nx * ny
    assert count > 1 and nz % 2 == 0 and wide == 128 and rhs % 16 == 0 and cols <= wide
    dma = pltpu.SemaphoreType.DMA
    vmem, anywhere = pl.BlockSpec(memory_space=pltpu.VMEM), pl.BlockSpec(memory_space=pl.ANY)
    turned, right, triangle = pl.pallas_call(
        functools.partial(kernel, (n_gx, n_gy, nx, ny, nz, unk, rhs)),
        out_shape=(
            jax.ShapeDtypeStruct((count, pairs, wide, 2 * wide), BF16),
            jax.ShapeDtypeStruct((2 * wide, 2 * wide), BF16),
            jax.ShapeDtypeStruct((cols, wide), F32),
        ),
        in_specs=[anywhere, vmem],
        out_specs=(vmem, vmem, vmem),
        scratch_shapes=[
            pltpu.VMEM((count, nz, 7, unk, unk), F32),
            pltpu.VMEM((count, pairs, 2, 2 * unk, 4 * wide), BF16),
            pltpu.VMEM((STEPS + 1, nx, ny, pairs, rhs, wide), F32),
            pltpu.VMEM((count, pairs, 2 * cols, wide), BF16),
            pltpu.VMEM((count, pairs + 2, 2, 2 * rhs, wide), BF16),
            pltpu.VMEM((count, pairs, wide, 2 * rhs), F32),
            pltpu.VMEM((STEPS, 2, ny, pairs, rhs, wide), F32),
            pltpu.VMEM((STEPS, 2, nx, pairs, rhs, wide), F32),
            pltpu.VMEM((3, n_gx, rhs, wide), F32),
            pltpu.VMEM((3, n_gy, rhs, wide), F32),
            dma((count,)),
            dma((STEPS, 2, ny)),
            dma((STEPS, 2, ny)),
            dma((STEPS, 2, nx)),
            dma((STEPS, 2, nx)),
            dma((3, n_gx)),
            dma((3, n_gx)),
            dma((3, n_gy)),
            dma((3, n_gy)),
        ],
        compiler_params=pltpu.CompilerParams(
            collective_id=0, has_side_effects=True, vmem_limit_bytes=50 * 1024 * 1024
        ),
        cost_estimate=pl.CostEstimate(flops=6_000_000_000, bytes_accessed=16_000_000, transcendentals=0),
    )(operator_blocks, jnp.swapaxes(start_block, -1, -2))
    return pl.pallas_call(
        functools.partial(product_kernel, (nx, ny, nz, unk, cols)),
        out_shape=(
            jax.ShapeDtypeStruct((nx, ny, nz, unk, cols), F32),
            jax.ShapeDtypeStruct((cols, cols), F32),
        ),
        in_specs=[vmem, vmem, vmem],
        out_specs=(anywhere, vmem),
        scratch_shapes=[pltpu.VMEM((count, nz, unk, cols), F32), dma((count,))],
        compiler_params=pltpu.CompilerParams(vmem_limit_bytes=24 * 1024 * 1024),
        cost_estimate=pl.CostEstimate(flops=400_000_000, bytes_accessed=4_000_000, transcendentals=0),
    )(turned, right, triangle)


def solution(mesh):
    in_specs = (P("gx", "gy", None, None, None, None), P("gx", "gy", None, None, None))
    out_specs = (P("gx", "gy", None, None, None), P())
    return jax.shard_map(
        per_device, mesh=mesh, in_specs=in_specs, out_specs=out_specs, check_vma=False
    )
```

```python
import functools

import jax
import jax.numpy as jnp
from jax import lax
from jax.experimental import pallas as pl
from jax.experimental.pallas import tpu as pltpu
from jax.sharding import PartitionSpec as P

STEPS = 4
F32 = jnp.float32
BF16 = jnp.bfloat16
NT = (((1,), (1,)), ((), ()))
MESH = pl.DeviceIdType.MESH


def limbs(value):
    high = value.astype(BF16)
    return high, (value - high.astype(F32)).astype(BF16)


def dot_nt(left, right):
    return lax.dot_general(left, right, NT, preferred_element_type=F32)


def chunk_of(count, most):
    return max(size for size in range(1, most + 1) if count % size == 0)


def dot_full(left, right, dims=(((1,), (0,)), ((), ()))):
    return lax.dot_general(left, right, dims, precision=lax.Precision.HIGHEST, preferred_element_type=F32)


def eliminate(blocks, start, stop):
    lane = lax.broadcasted_iota(jnp.int32, blocks[0].shape, 1)
    rows = lax.broadcasted_iota(jnp.int32, blocks[0].shape, 0)
    line = lane[:1]
    for j in range(start, stop, 2):
        first, inside = divmod(j, 8)
        row_0 = blocks[first][inside : inside + 1, :]
        row_1 = blocks[first][inside + 1 : inside + 2, :]
        a, b, c = row_0[:, j : j + 1], row_0[:, j + 1 : j + 2], row_1[:, j + 1 : j + 2]
        inverse = 1.0 / (a * c - b * b)
        unit_0 = jnp.where(line == j, 1.0, jnp.where(line == j + 1, 0.0, row_0))
        unit_1 = jnp.where(line == j + 1, 1.0, jnp.where(line == j, 0.0, row_1))
        scaled_0 = (c * unit_0 - b * unit_1) * inverse
        scaled_1 = (a * unit_1 - b * unit_0) * inverse
        ratio = b / a
        second = jnp.where(line == j, -ratio, row_1 - ratio * row_0)
        pair = jnp.logical_or(lane == j, lane == j + 1)
        for i in range(first, len(blocks)):
            block = blocks[i]
            kept = jnp.where(pair, 0.0, block)
            update = kept - block[:, j : j + 1] * scaled_0 - block[:, j + 1 : j + 2] * scaled_1
            if i == first:
                update = jnp.where(rows > inside + 1, update, jnp.where(rows == inside + 1, second, block))
            blocks[i] = update
        yield


def split_factor(blocks):
    factored = jnp.concatenate(blocks, axis=0)
    lane = lax.broadcasted_iota(jnp.int32, factored.shape, 1)
    rows = lax.broadcasted_iota(jnp.int32, factored.shape, 0)
    diagonal = jnp.sum(jnp.where(lane == rows, factored, 0.0), axis=1, keepdims=True)
    root = jnp.sqrt(diagonal)
    scale = 1.0 / root
    upper = jnp.where(lane > rows, factored * scale, jnp.where(lane == rows, root, 0.0))
    inverse = jnp.where(lane < rows, factored * scale, jnp.where(lane == rows, scale, 0.0))
    return upper, inverse


def kernel(dims, blocks_hbm, start_ref, turned, right_ref, tri_ref, raw, weights, tall, limb, mixed,
           partial, rx, ry, gram_x, gram_y, raw_sem, send_x, recv_x, send_y, recv_y, send_gx, recv_gx,
           send_gy, recv_gy):
    n_gx, n_gy, nx, ny, nz, unk, rhs = dims
    pairs = nz // 2
    wide = 2 * unk
    cols = (STEPS + 1) * rhs
    gx, gy = lax.axis_index("gx"), lax.axis_index("gy")
    columns = [(x, y) for x in range(nx) for y in range(ny)]
    chunk = chunk_of(pairs, 6)

    def raw_copy(c):
        x, y = columns[c]
        return pltpu.make_async_copy(blocks_hbm.at[x, y], raw.at[c], raw_sem.at[c])

    for c in range(len(columns)):
        raw_copy(c).start()

    barrier = pltpu.get_barrier_semaphore()
    for d in range(1, n_gx):
        pl.semaphore_signal(barrier, inc=1, device_id={"gx": lax.rem(gx + d, n_gx)}, device_id_type=MESH)
    for d in range(1, n_gy):
        pl.semaphore_signal(barrier, inc=1, device_id={"gy": lax.rem(gy + d, n_gy)}, device_id_type=MESH)

    def borders(c):
        x, y = columns[c]
        return [("gx", 0, x == 0), ("gx", 1, x == nx - 1), ("gy", 0, y == 0), ("gy", 1, y == ny - 1)]

    def order(c):
        marks = [edge for _, _, edge in borders(c)]
        return sorted(range(4), key=lambda d: marks[d])

    def neighbour(c, d):
        x, y = columns[c]
        x, y = x + (-1, 1, 0, 0)[d], y + (0, 0, -1, 1)[d]
        return columns.index((x, y)) if (x, y) in columns else None

    def store_basis(k, c, m, value):
        x, y = columns[c]
        tall[k, x, y, m] = value
        high, low = limbs(value)
        limb[c, m, rhs * k : rhs * (k + 1)] = high
        limb[c, m, cols + rhs * k : cols + rhs * (k + 1)] = low
        if k < STEPS:
            both = jnp.concatenate([high, low], axis=0)
            mixed[c, m, 1, :, 0:unk] = both[:, 0:unk]
            mixed[c, m + 2, 0, :, unk:wide] = both[:, unk:wide]
            for user in range(len(columns)):
                if neighbour(user, order(user)[0]) == c:
                    mixed[user, m + 1, 0, :, 0:unk] = both[:, 0:unk]
                    mixed[user, m + 1, 1, :, unk:wide] = both[:, unk:wide]

    def has(axis, side):
        here, count = (gx, n_gx) if axis == "gx" else (gy, n_gy)
        return here > 0 if side == 0 else here < count - 1

    def halo_copy(k, c, axis, side):
        x, y = columns[c]
        if axis == "gx":
            target, land, at, ss, rs = gx, rx, y, send_x, recv_x
        else:
            target, land, at, ss, rs = gy, ry, x, send_y, recv_y
        target = target - 1 if side == 0 else target + 1
        return pltpu.make_async_remote_copy(
            src_ref=tall.at[k, x, y], dst_ref=land.at[k, 1 - side, at],
            send_sem=ss.at[k, side, at], recv_sem=rs.at[k, 1 - side, at],
            device_id={axis: target}, device_id_type=MESH)

    def halo_wait(k, c, axis, side):
        x, y = columns[c]
        if axis == "gx":
            target, land, at, ss, rs = gx, rx, y, send_x, recv_x
        else:
            target, land, at, ss, rs = gy, ry, x, send_y, recv_y
        target = target - 1 if side == 0 else target + 1
        pltpu.make_async_remote_copy(
            src_ref=tall.at[k, x, y], dst_ref=land.at[k, side, at],
            send_sem=ss.at[k, side, at], recv_sem=rs.at[k, side, at],
            device_id={axis: target}, device_id_type=MESH).wait_recv()

    def send_column(k, c):
        for axis, side, edge in borders(c):
            if edge:
                @pl.when(has(axis, side))
                def _():
                    halo_copy(k, c, axis, side).start()

    for c, (x, y) in enumerate(columns):
        mixed[c, 1, 0, :, unk:wide] = jnp.zeros((2 * rhs, unk), BF16)
        mixed[c, pairs, 1, :, 0:unk] = jnp.zeros((2 * rhs, unk), BF16)
        for m in range(pairs):
            store_basis(0, c, m, jnp.concatenate([start_ref[x, y, 2 * m], start_ref[x, y, 2 * m + 1]], axis=1))
    for axis, land in (("gx", rx), ("gy", ry)):
        for side in (0, 1):
            @pl.when(jnp.logical_not(has(axis, side)))
            def _():
                for k in range(STEPS):
                    land[k, side] = jnp.zeros(land.shape[2:], F32)

    pl.semaphore_wait(barrier, n_gx + n_gy - 2)
    for c in range(len(columns)):
        send_column(0, c)

    def prepare(c):
        first, second, third, fourth = (1 + d for d in order(c))
        zeros = jnp.zeros((unk, unk), F32)

        for m in range(pairs):
            low, up = raw.at[c, 2 * m], raw.at[c, 2 * m + 1]
            halves = (
                ((low[0], low[6]), (low[first], low[5]), (low[third], low[fourth]), (low[second], zeros)),
                ((up[5], up[0]), (up[6], up[first]), (up[fourth], up[third]), (zeros, up[second])),
            )
            for half, pieces in enumerate(halves):
                for at, (left, right) in enumerate(pieces):
                    high, rest = limbs(jnp.concatenate([left, right], axis=1))
                    lanes = slice(at * wide, (at + 1) * wide)
                    weights[c, m, half, 0:unk, lanes] = high
                    weights[c, m, half, unk : 2 * unk, lanes] = rest

    def apply_tile(c, m, tile, operands):
        results = []
        for half in range(2):
            product = dot_nt(weights[c, m, half, :, 2 * wide * tile : 2 * wide * (tile + 1)], operands[half])
            results.append(product[0:unk] + product[unk : 2 * unk])
        return jnp.concatenate(results, axis=0)

    def rows_of(k, c, m):
        return jnp.concatenate(
            [limb[c, m, rhs * k : rhs * (k + 1)], limb[c, m, cols + rhs * k : cols + rhs * (k + 1)]], axis=0)

    def wait_halos(k, c):
        for axis, side, edge in borders(c):
            if edge:
                @pl.when(has(axis, side))
                def _():
                    halo_wait(k, c, axis, side)

    def near_part(k, c, beside=iter(())):
        for m in range(pairs):
            own = rows_of(k, c, m)
            operands = [jnp.concatenate([own, mixed[c, m + 1, half]], axis=1) for half in range(2)]
            partial[c, m] = apply_tile(c, m, 0, operands)
            next(beside, None)

    def far_part(k, c):
        x, y = columns[c]
        _, second, third, fourth = order(c)
        wait_halos(k, c)

        def values(d, m):
            other = neighbour(c, d)
            if other is None:
                return rx[k, d, y, m] if d < 2 else ry[k, d - 2, x, m]
            return tall[k, columns[other][0], columns[other][1], m]

        def body(i, carry):
            in_low = lax.broadcasted_iota(jnp.int32, (rhs, wide), 1) < unk
            for s in range(chunk):
                m = i * chunk + s
                if neighbour(c, second) is None:
                    alone = jnp.concatenate(limbs(values(second, m)), axis=0)
                else:
                    alone = rows_of(k, neighbour(c, second), m)
                plain, rolled = values(third, m), pltpu.roll(values(fourth, m), unk, 1)
                pairs_of = (jnp.where(in_low, plain, rolled), jnp.where(in_low, rolled, plain))
                operands = [
                    jnp.concatenate([jnp.concatenate(limbs(both), axis=0), alone], axis=1) for both in pairs_of]
                applied = (partial[c, m] + apply_tile(c, m, 1, operands)).T
                applied = applied[0:rhs] + applied[rhs : 2 * rhs]
                current = tall[k, x, y, m]
                if k == 0:
                    following = (applied - 8.0 * current) * (1.0 / 6.0)
                else:
                    following = (applied - 8.0 * current) * (2.0 / 6.0) - tall[k - 1, x, y, m]
                store_basis(k + 1, c, m, following)
            return carry

        lax.fori_loop(0, pairs // chunk, body, 0)

    def gram_rows(begin, end):
        count, size = rhs * end, rhs * (end - begin)
        total_high = jnp.zeros((2 * size, count), F32)
        total_low = jnp.zeros((2 * size, count), F32)
        for c in range(len(columns)):
            for m in range(0, pairs, 2):
                span = range(m, min(m + 2, pairs))
                high = jnp.concatenate([limb[c, q, 0:count] for q in span], axis=1)
                low = jnp.concatenate([limb[c, q, cols : cols + count] for q in span], axis=1)
                left = jnp.concatenate([high[count - size :], low[count - size :]], axis=0)
                total_high += dot_nt(left, high)
                total_low += dot_nt(left, low)
        total = total_high + total_low
        return total[0:size] + total[size : 2 * size]

    axes = {"gx": (gx, n_gx, gram_x, send_gx, recv_gx), "gy": (gy, n_gy, gram_y, send_gy, recv_gy)}
    early = STEPS - 1
    assert rhs * early * (early + 1) // 2 <= wide

    def put_gram(part, values):
        values = list(values)
        used = sum(value.shape[1] for value in values)
        if used < wide:
            values.append(jnp.zeros((rhs, wide - used), F32))
        gram_x[part, gx] = jnp.concatenate(values, axis=1)

    def gram_copy(axis, k, d, receive=False):
        here, count, slots, send, recv = axes[axis]
        other = lax.rem(here + d, count)
        slot = other if receive else here
        return pltpu.make_async_remote_copy(
            src_ref=slots.at[k, slot], dst_ref=slots.at[k, slot], send_sem=send.at[k, d],
            recv_sem=recv.at[k, slot], device_id={axis: other}, device_id_type=MESH)

    def gram_send(axis, k):
        for d in range(1, axes[axis][1]):
            gram_copy(axis, k, d).start()

    def gram_sum(axis, k):
        _, count, slots, _, _ = axes[axis]
        for d in range(1, count):
            gram_copy(axis, k, d, receive=True).wait_recv()
        total = slots[k, 0]
        for i in range(1, count):
            total = total + slots[k, i]
        return total

    def gram_turn(k):
        gram_y[k, gy] = gram_sum("gx", k)
        gram_send("gy", k)

    def lanes_from(value, begin, count):
        return jnp.concatenate([value[:, begin : begin + count], jnp.zeros((rhs, wide - count), F32)], axis=1)

    def append(known, norm, rows_value, at):
        rows = lax.broadcasted_iota(jnp.int32, (rhs, wide), 0)
        lane = lax.broadcasted_iota(jnp.int32, (rhs, wide), 1)
        on_diagonal = jnp.where(lane == rows + at, rows_value, 0.0)
        norm_rows = jnp.sqrt(jnp.sum(on_diagonal, axis=1, keepdims=True))
        norm = jnp.where(line // rhs == at // rhs, jnp.sqrt(jnp.sum(on_diagonal, axis=0, keepdims=True)), norm)
        scaled = rows_value / (norm_rows * norm)
        full = jnp.concatenate([known, jnp.zeros((wide - at, wide), F32)], axis=0)
        side = dot_full(jnp.where(lane < at, scaled, 0.0), full, NT)
        rest = scaled[:, at : at + rhs] - dot_full(side, side, NT)
        rest = lanes_from(rest, 0, rhs)
        rest = [rest[8 * i : 8 * i + 8] for i in range(rhs // 8)]
        for _ in eliminate(rest, 0, rhs):
            pass
        upper, inverse = split_factor(rest)
        below = dot_full(inverse[:, 0:rhs], dot_full(side, full))

        def placed(value):
            pieces = [jnp.zeros((rhs, at), F32), value[:, 0:rhs], jnp.zeros((rhs, wide - at - rhs), F32)]
            return jnp.concatenate([piece for piece in pieces if piece.shape[1]], axis=1)

        known = jnp.concatenate([known, placed(inverse) - below], axis=0)
        beside = jnp.concatenate(
            [jnp.zeros((at, wide), F32), side, jnp.zeros((wide - at - rhs, wide), F32)], axis=0).T
        return known, norm, placed(upper), beside[0:at]

    front = early * rhs
    rows = lax.broadcasted_iota(jnp.int32, (front, wide), 0)
    lane = lax.broadcasted_iota(jnp.int32, (front, wide), 1)
    line = lane[:1]

    def first_rows():
        total = gram_sum("gy", 0)
        pieces, begin = [], 0
        for k in range(early):
            pieces.append(lanes_from(total, begin, rhs * (k + 1)))
            begin += rhs * (k + 1)
        lower = jnp.concatenate(pieces, axis=0)
        square = jnp.concatenate([lower, jnp.zeros((wide - front, wide), F32)], axis=0)
        whole = jnp.where(lane > rows, square.T[0:front], lower)
        on_diagonal = jnp.where(lane == rows, whole, 0.0)
        norm_rows = jnp.sqrt(jnp.sum(on_diagonal, axis=1, keepdims=True))
        norm = jnp.where(line < front, jnp.sqrt(jnp.sum(on_diagonal, axis=0, keepdims=True)), 1.0)
        whole = whole / (norm_rows * norm)
        return [whole[8 * i : 8 * i + 8] for i in range(front // 8)], norm

    for c in range(len(columns)):
        raw_copy(c).wait()
        prepare(c)
        near_part(0, c)
    for k in range(STEPS):
        pivots = iter(())
        if k == early - 1:
            products = gram_rows(0, early)
            put_gram(0, [products[rhs * i : rhs * (i + 1), 0 : rhs * (i + 1)] for i in range(early)])
            gram_send("gx", 0)
        if k == early:
            put_gram(1, [gram_rows(early, STEPS)])
            gram_send("gx", 1)
            blocks, norm = first_rows()
            pivots = eliminate(blocks, 0, front)
        if k > 0:
            for c in range(len(columns)):
                near_part(k, c, pivots)
        for _ in pivots:
            pass
        if k == early - 1:
            gram_turn(0)
        for c in range(len(columns)):
            far_part(k, c)
            if k + 1 < STEPS:
                send_column(k + 1, c)
    gram_turn(1)
    put_gram(2, [gram_rows(STEPS, STEPS + 1)])
    gram_send("gx", 2)

    for c, (x, y) in enumerate(columns):
        for m in range(pairs):
            pieces = [tall[k, x, y, m] for k in range(STEPS + 1)]
            block = jnp.concatenate(pieces + [jnp.zeros((wide - cols, wide), F32)], axis=0).T
            turned[c, m] = jnp.concatenate(limbs(block), axis=1)

    upper, known = split_factor(blocks)
    fourth_rows = gram_sum("gy", 1)
    gram_turn(2)
    known, norm, upper_3, beside_3 = append(known, norm, fourth_rows, front)
    known, norm, upper_4, beside_4 = append(known, norm, gram_sum("gy", 2), front + rhs)
    triangle = jnp.concatenate([upper + beside_3, upper_3], axis=0) + beside_4
    triangle = jnp.concatenate([triangle, upper_4], axis=0) * norm
    tri_ref[...] = triangle
    inverse = jnp.concatenate([known, jnp.zeros((wide - cols, wide), F32)], axis=0) / norm
    high, low = limbs(inverse)
    right_ref[0:wide, 0:wide] = high
    right_ref[0:wide, wide : 2 * wide] = high
    right_ref[wide : 2 * wide, 0:wide] = low
    right_ref[wide : 2 * wide, wide : 2 * wide] = low

    for k in range(3):
        for axis in axes:
            for d in range(1, axes[axis][1]):
                gram_copy(axis, k, d).wait_send()
    for k in range(STEPS):
        for c in range(len(columns)):
            for axis, side, edge in borders(c):
                if edge:
                    @pl.when(has(axis, side))
                    def _():
                        halo_copy(k, c, axis, side).wait_send()


def product_kernel(dims, turned, right_ref, tri_in, ortho_hbm, tri_ref, ortho, ortho_sem):
    nx, ny, nz, unk, cols = dims
    wide = 2 * unk
    columns = [(x, y) for x in range(nx) for y in range(ny)]
    tri_ref[...] = tri_in[:, 0:cols]

    def ortho_copy(c):
        x, y = columns[c]
        return pltpu.make_async_copy(ortho.at[c], ortho_hbm.at[x, y], ortho_sem.at[c])

    for c in range(len(columns)):
        for m in range(nz // 2):
            product = dot_nt(turned[c, m], right_ref[...])
            result = (product[:, 0:wide] + product[:, wide : 2 * wide])[:, 0:cols]
            ortho[c, 2 * m] = result[0:unk]
            ortho[c, 2 * m + 1] = result[unk:wide]
        ortho_copy(c).start()
    for c in range(len(columns)):
        ortho_copy(c).wait()


def per_device(operator_blocks, start_block):
    nx, ny, nz, _, unk, _ = operator_blocks.shape
    rhs = start_block.shape[-1]
    n_gx, n_gy = lax.axis_size("gx"), lax.axis_size("gy")
    pairs, wide, cols, count = nz // 2, 2 * unk, (STEPS + 1) * rhs, nx * ny
    assert count > 1 and nz % 2 == 0 and wide == 128 and rhs % 16 == 0 and cols <= wide
    dma = pltpu.SemaphoreType.DMA
    vmem, anywhere = pl.BlockSpec(memory_space=pltpu.VMEM), pl.BlockSpec(memory_space=pl.ANY)
    turned, right, triangle = pl.pallas_call(
        functools.partial(kernel, (n_gx, n_gy, nx, ny, nz, unk, rhs)),
        out_shape=(
            jax.ShapeDtypeStruct((count, pairs, wide, 2 * wide), BF16),
            jax.ShapeDtypeStruct((2 * wide, 2 * wide), BF16),
            jax.ShapeDtypeStruct((cols, wide), F32),
        ),
        in_specs=[anywhere, vmem],
        out_specs=(vmem, vmem, vmem),
        scratch_shapes=[
            pltpu.VMEM((count, nz, 7, unk, unk), F32),
            pltpu.VMEM((count, pairs, 2, 2 * unk, 4 * wide), BF16),
            pltpu.VMEM((STEPS + 1, nx, ny, pairs, rhs, wide), F32),
            pltpu.VMEM((count, pairs, 2 * cols, wide), BF16),
            pltpu.VMEM((count, pairs + 2, 2, 2 * rhs, wide), BF16),
            pltpu.VMEM((count, pairs, wide, 2 * rhs), F32),
            pltpu.VMEM((STEPS, 2, ny, pairs, rhs, wide), F32),
            pltpu.VMEM((STEPS, 2, nx, pairs, rhs, wide), F32),
            pltpu.VMEM((3, n_gx, rhs, wide), F32),
            pltpu.VMEM((3, n_gy, rhs, wide), F32),
            dma((count,)),
            dma((STEPS, 2, ny)),
            dma((STEPS, 2, ny)),
            dma((STEPS, 2, nx)),
            dma((STEPS, 2, nx)),
            dma((3, n_gx)),
            dma((3, n_gx)),
            dma((3, n_gy)),
            dma((3, n_gy)),
        ],
        compiler_params=pltpu.CompilerParams(
            collective_id=0, has_side_effects=True, vmem_limit_bytes=50 * 1024 * 1024
        ),
        cost_estimate=pl.CostEstimate(flops=6_000_000_000, bytes_accessed=16_000_000, transcendentals=0),
    )(operator_blocks, jnp.swapaxes(start_block, -1, -2))
    return pl.pallas_call(
        functools.partial(product_kernel, (nx, ny, nz, unk, cols)),
        out_shape=(
            jax.ShapeDtypeStruct((nx, ny, nz, unk, cols), F32),
            jax.ShapeDtypeStruct((cols, cols), F32),
        ),
        in_specs=[vmem, vmem, vmem],
        out_specs=(anywhere, vmem),
        scratch_shapes=[pltpu.VMEM((count, nz, unk, cols), F32), dma((count,))],
        compiler_params=pltpu.CompilerParams(vmem_limit_bytes=24 * 1024 * 1024),
        cost_estimate=pl.CostEstimate(flops=400_000_000, bytes_accessed=4_000_000, transcendentals=0),
    )(turned, right, triangle)


def solution(mesh):
    in_specs = (P("gx", "gy", None, None, None, None), P("gx", "gy", None, None, None))
    out_specs = (P("gx", "gy", None, None, None), P())
    return jax.shard_map(
        per_device, mesh=mesh, in_specs=in_specs, out_specs=out_specs, check_vma=False
    )
```
